256 devices in a mesh: pt: 8 (over y, core), row: 8 (over z), col: 4 (over x).
Axes of the slice: x: 4, y: 4, z: 8, core: 2. Of those that a mesh axis runs over, the one named last changes fastest.
Arguments:
- jac_cam: float32 [8, 2, 9, 524288], P(None, None, None, ('pt', 'row', 'col')), may hold values from -6 to 6
- jac_pt: float32 [8, 2, 3, 524288], P(None, None, None, ('pt', 'row', 'col')), may hold values from -6 to 6
- obs_cam: int32 [8, 524288], P(None, ('pt', 'row', 'col')), may hold values from 0 to 63
- point_covisible_tile: int32 [524288, 1], P(('pt', 'row', 'col')), may hold values from 0 to 31; in each aligned block of 2048 rows (0 to 2047, 2048 to 4095, ...) at most 128 rows name the same one
Outputs:
- upper_schur_tiles: float32 [32, 576, 576], P(('row', 'col'), 'pt')
- lower_tiles: float32 [32, 576, 576], P(('row', 'col'), 'pt')
The draws below stay inside these ranges and needn't reach their ends.
Inputs may be any that keep to these rules, and one draw needn't show every extreme that they name: `point_covisible_tile`: among the 2048 points of one device no tile is named by more than 128 points, a bound that some block reaches.
All inputs are finite; a program needn't handle non-finite values.
Results may differ from the reference program's by a relative error of at most 0.0047.
Values sent between devices are 32-bit elements; how exact they have to be, the bound alone decides.
A program may use at most 64 MiB of HBM per device.

```python
import math
import jax
import jax.numpy as jnp
import numpy as np
from jax import lax

CAMB = 64
OBS = 8
POINTS_PER_UNIT = 2048
COVISIBLE_TILES = 32
TILE_POINT_LIMIT = 128
WINDOW_POINTS = 524288
N_PT = 8
N_ROW = 8
N_COL = 4


def plant(array, rng, low, top_value):
    dims = array.shape
    place = [jax.random.randint(jax.random.fold_in(rng, axis), (), 0, dims[axis]) for axis in range(len(dims))]
    array = array.at[tuple(place)].set(low)
    longest = dims.index(max(dims))
    place[longest] = (place[longest] + 1) % dims[longest]
    return array.at[tuple(place)].set(top_value)


def levels(rng, shape, shards, smallest, largest):
    gain, own = 1.0, jax.random.fold_in(rng, 6)
    for dim, parts in shards:
        draws = jnp.exp(jax.random.uniform(jax.random.fold_in(own, dim), (parts,), jnp.float32, smallest / len(shards), largest / len(shards)))
        gain = gain * jnp.repeat(draws, shape[dim] // parts).reshape([-1 if axis == dim else 1 for axis in range(len(shape))])
    return gain


def routed_block(own_key, own, number, rows, count, top, most, lean):
    sequence = jax.random.permutation(own_key, count)
    crowded, common = shares(count, rows * top, most, lean, True), shares(count, rows * top, most, lean, False)
    places = jnp.arange(count)

    def named(sizes, turn):
        used = int((sizes > 0).sum())
        fixed = max(1, used // 4)
        passed = fixed + (places - fixed + turn * (used - fixed)) % max(1, count - fixed)
        return jnp.zeros((count,), jnp.int32).at[sequence[jnp.where(places < fixed, places, passed)]].set(jnp.asarray(sizes, jnp.int32))

    sizes = jnp.where(number % 4 == 0, named(crowded, number // 4), named(common, number - number // 4 - 1))
    mixed = jax.random.permutation(jax.random.fold_in(own, 3), count)
    source_of, receiver = mixed[0:count // 2 * 2:2], mixed[1:count // 2 * 2:2]
    room = jnp.minimum(sizes[source_of] - 1, most - sizes[receiver]) // 2
    room = jnp.where((source_of == sequence[0]) | (receiver == sequence[0]) | (sizes[receiver] == 0), 0, jnp.maximum(room, 0))
    passed = jax.random.randint(jax.random.fold_in(own, 4), (count // 2,), 0, 1 << 20) % (room + 1)
    sizes = sizes.at[source_of].add(-passed).at[receiver].add(passed)
    items = jnp.searchsorted(jnp.cumsum(sizes), jnp.arange(rows * top), side="right").astype(jnp.int32)
    grid = items.reshape(top, rows).T
    grid = grid[jax.random.permutation(jax.random.fold_in(own, 1), rows)]
    turn = jax.random.randint(jax.random.fold_in(own, 2), (rows, 1), 0, top)
    return jnp.take_along_axis(grid, (jnp.arange(top)[None, :] + turn) % top, axis=1)


def shares(amount, total, bound, slope, full):
    weights = [(1 << 20) // math.isqrt(standing ** slope) + 1 for standing in range(1, amount + 1)]
    largest = bound if full else min(bound, max(-(-total // amount), total * weights[0] // sum(weights)))
    least = 1 if total - largest >= amount - 1 else 0
    holding, surplus = [largest] + [least] * (amount - 1), total - largest - least * (amount - 1)
    while surplus > 0:
        candidates = [i for i in range(1, amount) if holding[i] < largest] or [i for i in range(1, amount) if holding[i] < bound]
        mass, left = sum([weights[i] for i in candidates]), surplus
        for i in candidates:
            addition = min(bound - holding[i], max(1, left * weights[i] // mass), surplus)
            holding[i] = holding[i] + addition
            surplus = surplus - addition
    return np.array(holding)


def centred(key, shape, spread, limit, cuts=(), kind=jnp.bfloat16):
    level = levels(key, shape, cuts, -0.22, 0.18) if cuts else 1.0
    entries = jax.random.normal(key, shape, jnp.float32) * spread * level
    return jnp.minimum(jnp.maximum(entries, -limit), limit).astype(kind)


def setup_inputs(seed: int = 0) -> dict:
    key_of = jax.random.split(jax.random.key(seed), 5)
    jac_cam = centred(key_of[0], (OBS, 2, 9, WINDOW_POINTS), 1.0, 6.0, ((3, 256),), jnp.float32)
    jac_pt = centred(key_of[1], (OBS, 2, 3, WINDOW_POINTS), 1.0, 6.0, ((3, 256),), jnp.float32)
    obs_cam = plant(jax.random.randint(key_of[2], (OBS, WINDOW_POINTS), 0, CAMB), jax.random.fold_in(key_of[2], 1), 0, CAMB - 1).astype(jnp.int32)
    point_covisible_tile_keys = jax.random.split(jax.random.fold_in(key_of[3], 1), WINDOW_POINTS // POINTS_PER_UNIT)
    point_covisible_tile_turns = jax.random.permutation(jax.random.fold_in(key_of[3], 3), WINDOW_POINTS // POINTS_PER_UNIT)
    point_covisible_tile = jax.vmap(lambda own, number: routed_block(jax.random.fold_in(key_of[3], 2), own, number, POINTS_PER_UNIT, COVISIBLE_TILES, 1, TILE_POINT_LIMIT, 2))(point_covisible_tile_keys, point_covisible_tile_turns).reshape((WINDOW_POINTS, 1))
    return {"jac_cam": jac_cam, "jac_pt": jac_pt, "obs_cam": obs_cam, "point_covisible_tile": point_covisible_tile}


DAMPING = 1.0


def inverse_entries(point_jac):
    normal_matrix = [[None, None, None], [None, None, None], [None, None, None]]
    for first in range(3):
        for second in range(first, 3):
            element = jnp.sum(point_jac[:, :, first, :] * point_jac[:, :, second, :], axis=(0, 1))
            if first == second:
                element = element + DAMPING
            normal_matrix[first][second] = element
            normal_matrix[second][first] = element
    vzz = normal_matrix[0][0]
    vzo = normal_matrix[0][1]
    vzt = normal_matrix[0][2]
    voo = normal_matrix[1][1]
    vot = normal_matrix[1][2]
    vtt = normal_matrix[2][2]
    adj_zz = voo * vtt - vot * vot
    adj_zo = vzt * vot - vzo * vtt
    adj_zt = vzo * vot - vzt * voo
    adj_oo = vzz * vtt - vzt * vzt
    adj_ot = vzo * vzt - vzz * vot
    adj_tt = vzz * voo - vzo * vzo
    determinant = vzz * adj_zz + vzo * adj_zo + vzt * adj_zt
    reciprocal = 1.0 / determinant
    adjugate = [[adj_zz, adj_zo, adj_zt], [adj_zo, adj_oo, adj_ot], [adj_zt, adj_ot, adj_tt]]
    return jnp.stack([jnp.stack(line, 0) for line in adjugate], 0) * reciprocal[None, None, :]


def tile_factors(camera_jac, point_jac, cameras):
    points = camera_jac.shape[-1]
    halfway = camera_jac.shape[0] // 2
    inverse = inverse_entries(point_jac)
    cross_terms = jnp.sum(camera_jac[:, :, :, None, :] * point_jac[:, :, None, :, :], axis=1)
    scaled = jnp.sum(cross_terms[:, :, :, None, :] * inverse[None, None, :, :, :], axis=2)
    labels = jnp.arange(CAMB, dtype=jnp.int32)[:, None, None, None]
    left_factor = jnp.zeros((CAMB, 9, 3, points), jnp.float32)
    right_factor = jnp.zeros((CAMB, 9, 3, points), jnp.float32)
    for obs_index in range(halfway):
        left_factor = left_factor + jnp.where(cameras[obs_index][None, None, None, :] == labels, scaled[obs_index][None], 0.0)
        right_factor = right_factor + jnp.where(cameras[halfway + obs_index][None, None, None, :] == labels, cross_terms[halfway + obs_index][None], 0.0)
    left_factor = left_factor.reshape(CAMB * 9, 3 * points).astype(jnp.bfloat16)
    right_factor = right_factor.reshape(CAMB * 9, 3 * points).astype(jnp.bfloat16)
    return left_factor, right_factor


def reference(jac_cam, jac_pt, obs_cam, point_covisible_tile):
    overall = jac_cam.shape[-1]
    slot_total = N_PT * N_ROW * N_COL * TILE_POINT_LIMIT
    block_size = math.gcd(2048, slot_total)
    camera_all = jnp.concatenate([jac_cam, jnp.zeros(jac_cam.shape[:-1] + (1,), jnp.float32)], axis=-1)
    point_all = jnp.concatenate([jac_pt, jnp.zeros(jac_pt.shape[:-1] + (1,), jnp.float32)], axis=-1)
    camera_ids = jnp.concatenate([obs_cam, jnp.zeros((obs_cam.shape[0], 1), jnp.int32)], axis=-1)
    tile_ids = point_covisible_tile[:, 0]

    def single_tile(slot):
        chosen = jnp.nonzero(tile_ids == slot, size=slot_total, fill_value=overall)[0].astype(jnp.int32)

        def accumulate(partial_value, first_point):
            picked = lax.dynamic_slice_in_dim(chosen, first_point, block_size)
            camera_jac = jnp.take(camera_all, picked, axis=3)
            point_jac = jnp.take(point_all, picked, axis=3)
            cameras = jnp.take(camera_ids, picked, axis=1)
            left_factor, right_factor = tile_factors(camera_jac, point_jac, cameras)
            product = lax.dot_general(left_factor, right_factor, (((1,), (1,)), ((), ())), preferred_element_type=jnp.float32)
            return partial_value - product, None

        starts = jnp.arange(slot_total // block_size, dtype=jnp.int32) * block_size
        partial_value, _unused = lax.scan(accumulate, jnp.zeros((9 * CAMB, 9 * CAMB), jnp.float32), starts)
        return partial_value

    upper_schur_tiles = lax.map(single_tile, jnp.arange(COVISIBLE_TILES, dtype=jnp.int32))
    paired_camera = jnp.bitwise_xor(jnp.arange(COVISIBLE_TILES, dtype=jnp.int32), COVISIBLE_TILES // 2)
    lower_tiles = jnp.transpose(upper_schur_tiles[paired_camera], (0, 2, 1))
    return upper_schur_tiles, lower_tiles
```

```python
import functools

import jax
import jax.numpy as jnp
from jax import lax
from jax.experimental import pallas as pl
from jax.experimental.pallas import tpu as pltpu
from jax.sharding import PartitionSpec as P

F32 = jnp.float32
BF16 = jnp.bfloat16
MESH = pl.DeviceIdType.MESH

CAMB = 64
DAMPING = 1.0
LANES = 128
TILES = 32
FEATURES = 200
PT_ROW = 144
CAM_ROW = 192
GROUP = 4
WIDTH = 9 * CAMB
NT = (((1,), (1,)), ((), ()))
SPLIT = (0, 5, 9)


def point_factors(pt_ref, out_ref):
    def entry(obs, coordinate, residual):
        return pt_ref[pl.ds((obs * 3 + coordinate) * 32 + residual, 16, stride=2), :]

    sums = {}
    for first in range(3):
        for second in range(first, 3):
            total = None
            for obs in range(8):
                for residual in range(2):
                    term = entry(obs, first, residual) * entry(obs, second, residual)
                    total = term if total is None else total + term
            sums[first, second] = total + DAMPING if first == second else total
    vzz, vzo, vzt = sums[0, 0], sums[0, 1], sums[0, 2]
    voo, vot, vtt = sums[1, 1], sums[1, 2], sums[2, 2]
    adj_zz = voo * vtt - vot * vot
    adj_zo = vzt * vot - vzo * vtt
    adj_zt = vzo * vot - vzt * voo
    adj_oo = vzz * vtt - vzt * vzt
    adj_ot = vzo * vzt - vzz * vot
    adj_tt = vzz * voo - vzo * vzo
    reciprocal = 1.0 / (vzz * adj_zz + vzo * adj_zo + vzt * adj_zt)
    inverse = [
        [entry_ * reciprocal for entry_ in line]
        for line in ((adj_zz, adj_zo, adj_zt), (adj_zo, adj_oo, adj_ot), (adj_zt, adj_ot, adj_tt))
    ]
    for residual in range(2):
        for obs in range(8):
            parts = [entry(obs, coordinate, residual) for coordinate in range(3)]
            for coordinate in range(3):
                if obs < 4:
                    value = (
                        parts[0] * inverse[0][coordinate]
                        + parts[1] * inverse[1][coordinate]
                        + parts[2] * inverse[2][coordinate]
                    )
                else:
                    value = parts[coordinate]
                row = (residual * 24 + obs * 3 + coordinate) * 16
                out_ref[row : row + 16, :] = value


def ranks(tile_ref, member_ref, rank_ref):
    for block in range(16):
        ids = jnp.broadcast_to(tile_ref[block : block + 1, :], (TILES, LANES))
        same = ids == lax.broadcasted_iota(jnp.int32, (TILES, LANES), 0)
        member_ref[block * TILES : (block + 1) * TILES, :] = jnp.where(same, 1.0, 0.0).astype(BF16)
    rows = lax.broadcasted_iota(jnp.int32, (LANES, LANES), 0)
    columns = lax.broadcasted_iota(jnp.int32, (LANES, LANES), 1)
    earlier = jnp.where(rows < columns, 1.0, 0.0).astype(BF16)
    members = member_ref[...]
    before = jnp.dot(members, earlier, preferred_element_type=F32)
    totals = jnp.dot(members, jnp.ones((LANES, LANES), BF16), preferred_element_type=F32)
    base = jnp.zeros((TILES, LANES), F32)
    for block in range(16):
        span = slice(block * TILES, (block + 1) * TILES)
        own = members[span].astype(F32) * (before[span] + base)
        rank_ref[block : block + 1, :] = jnp.sum(own, axis=0, keepdims=True)
        base = base + totals[span]


def gather_features(cam_ref, factor_ref, obs_ref, x_ref):
    for block in range(16):
        lanes = slice(block * LANES, (block + 1) * LANES)
        parts = [cam_ref[pl.ds(block * 2 + residual, 72, stride=32), :] for residual in range(2)]
        parts.append(factor_ref[pl.ds(block, 48, stride=16), :])
        values = jnp.concatenate(parts, axis=0)
        high = values.astype(BF16)
        x_ref[0:192, lanes] = high
        x_ref[208:400, lanes] = (values - high.astype(F32)).astype(BF16)
        names = obs_ref[:, lanes].astype(F32) + 1.0
        x_ref[192:208, lanes] = jnp.concatenate([names, jnp.zeros((8, LANES), F32)], axis=0).astype(BF16)


def place_points(x_ref, tile_ref, rank_ref, place_ref, wanted):
    slots = lax.broadcasted_iota(jnp.int32, (LANES, LANES), 0).astype(F32).astype(BF16)
    one, zero = jnp.ones((LANES, LANES), BF16), jnp.zeros((LANES, LANES), BF16)
    for part in range(2):
        slot_of = jnp.where(tile_ref[...] == wanted[part], rank_ref[...], -1.0)
        for block in range(16):
            row = jnp.broadcast_to(slot_of[block : block + 1, :], (LANES, LANES)).astype(BF16)
            place_ref[part * LANES : (part + 1) * LANES, block * LANES : (block + 1) * LANES] = jnp.where(
                row == slots, one, zero
            )
    placed = lax.dot_general(x_ref[...], place_ref[...], NT, preferred_element_type=F32)
    return placed[0:192] + placed[208:400], placed[192:200]


def fill_factor(block_ref, half, factor_ref, position):
    labels = (lax.broadcasted_iota(jnp.int32, (CAMB, LANES), 0).astype(F32) + 1.0).astype(BF16)
    cameras, masks, cross = [], [], []
    for index in range(4):
        obs = 4 * half + index
        camera = block_ref[CAM_ROW + obs : CAM_ROW + obs + 1, :]
        cameras.append(camera)
        masks.append(labels == jnp.broadcast_to(camera, (CAMB, LANES)).astype(BF16))
        camera_rows = [block_ref[res * 72 + obs * 9 : res * 72 + obs * 9 + 9, :] for res in range(2)]
        line = []
        for coordinate in range(3):
            rows = [PT_ROW + res * 24 + obs * 3 + coordinate for res in range(2)]
            line.append(
                camera_rows[0] * block_ref[rows[0] : rows[0] + 1, :]
                + camera_rows[1] * block_ref[rows[1] : rows[1] + 1, :]
            )
        cross.append(line)
    for index in range(4):
        for later in range(index + 1, 4):
            same = cameras[index] == cameras[later]
            for coordinate in range(3):
                cross[index][coordinate] = cross[index][coordinate] + jnp.where(same, cross[later][coordinate], 0.0)
    for coordinate in range(3):
        first = (coordinate * GROUP + position) * LANES
        for parameter in range(9):
            value = jnp.zeros((CAMB, LANES), BF16)
            for index in (3, 2, 1, 0):
                row = cross[index][coordinate][parameter : parameter + 1, :]
                value = jnp.where(masks[index], jnp.broadcast_to(row, (CAMB, LANES)).astype(BF16), value)
            factor_ref[parameter * CAMB : (parameter + 1) * CAMB, first : first + LANES] = value


def split_three(value):
    high = value.astype(BF16)
    rest = value - high.astype(F32)
    middle = rest.astype(BF16)
    return high, middle, (rest - middle.astype(F32)).astype(BF16)


def kernel(
    cam_ref, pt_ref, obs_ref, tile_ref, upper_ref, lower_ref,
    x_ref, factor_ref, member_ref, rank_ref, place_ref, sent_ref, held_ref, left_ref, right_ref,
    total_ref, ring_a, ring_b, perm_ref, rows_ref, share_ref, flip_ref, blocks_ref,
    sent_sem, held_sem, ring_sent, ring_held, share_sem, flip_sent, flip_held,
):
    pt, row, col = lax.axis_index("pt"), lax.axis_index("row"), lax.axis_index("col")
    y, core = pt // 2, lax.rem(pt, 2)
    mirror = lax.rem(row + 4, 8)
    same = (pt == row).astype(jnp.int32)
    flip_self = (pt == mirror).astype(jnp.int32)

    def chip_at(pair):
        return lax.rem(y + pair // 4, 4), lax.rem(col + lax.rem(pair, 4), 4)

    def core_at(part):
        return core if part == 0 else 1 - core

    barrier = pltpu.get_barrier_semaphore()

    def greet(pair, _):
        there_y, there_x = chip_at(pair)
        for part in range(2):
            pl.semaphore_signal(
                barrier, inc=1, device_id=(there_y * 2 + core_at(part), row, there_x), device_id_type=MESH
            )
        return 0

    lax.fori_loop(1, 16, greet, 0)
    pl.semaphore_signal(barrier, inc=1, device_id=(y * 2 + 1 - core, row, col), device_id_type=MESH)
    ahead, behind = lax.rem(row + 1, 8), lax.rem(row + 7, 8)
    pl.semaphore_signal(barrier, inc=1, device_id=(pt, ahead, col), device_id_type=MESH)
    pl.semaphore_signal(barrier, inc=1, device_id=(pt, behind, col), device_id_type=MESH)

    @pl.when(same == 0)
    def _():
        pl.semaphore_signal(barrier, inc=1, device_id=(row, pt, col), device_id_type=MESH)

    def greet_flip(other, _):
        @pl.when((pt != mirror) | (row != other))
        def _():
            pl.semaphore_signal(barrier, inc=1, device_id=(mirror, other, col), device_id_type=MESH)

        return 0

    lax.fori_loop(0, 8, greet_flip, 0)

    point_factors(pt_ref, factor_ref)
    ranks(tile_ref, member_ref, rank_ref)
    gather_features(cam_ref, factor_ref, obs_ref, x_ref)

    pl.semaphore_wait(barrier, 31 + 2 + (1 - same) + 8 - flip_self)

    def dispatch(index, there):
        return pltpu.make_async_remote_copy(
            src_ref=sent_ref.at[index],
            dst_ref=held_ref.at[index],
            send_sem=sent_sem.at[index],
            recv_sem=held_sem.at[index],
            device_id=there,
            device_id_type=MESH,
        )

    def send_pair(pair, _):
        there_y, there_x = chip_at(pair)
        owners = [there_y * 2 + core_at(part) for part in range(2)]
        placed, names = place_points(
            x_ref, tile_ref, rank_ref, place_ref, [owner * 4 + there_x for owner in owners]
        )
        for part in range(2):
            lanes = slice(part * LANES, (part + 1) * LANES)
            sent_ref[2 * pair + part, 0:192, :] = placed[:, lanes]
            sent_ref[2 * pair + part, 192:200, :] = names[:, lanes]
            dispatch(2 * pair + part, (owners[part], row, there_x)).start()
        return 0

    lax.fori_loop(1, 16, send_pair, 0)
    sibling = y * 2 + 1 - core
    placed, names = place_points(x_ref, tile_ref, rank_ref, place_ref, [pt * 4 + col, sibling * 4 + col])
    sent_ref[1, 0:192, :] = placed[:, LANES:]
    sent_ref[1, 192:200, :] = names[:, LANES:]
    dispatch(1, (sibling, row, col)).start()
    held_ref[0, 0:192, :] = placed[:, :LANES]
    held_ref[0, 192:200, :] = names[:, :LANES]

    source = lax.broadcasted_iota(jnp.int32, (WIDTH, WIDTH), 1)
    goal = lax.broadcasted_iota(jnp.int32, (WIDTH, WIDTH), 0)
    target = (source & 63) * 9 + (source >> 6)
    perm_ref[...] = jnp.where(target == goal, 1.0, 0.0).astype(BF16)

    total_ref[...] = jnp.zeros_like(total_ref)

    def add_group(group, _):
        for position in range(GROUP):
            index = group * GROUP + position

            @pl.when(index > 0)
            def _():
                dispatch(index, (pt, row, col)).wait_recv()

        for position in range(GROUP):
            block = held_ref.at[group * GROUP + position]
            fill_factor(block, 0, left_ref, position)
            fill_factor(block, 1, right_ref, position)
        product = lax.dot_general(left_ref[...], right_ref[...], NT, preferred_element_type=F32)
        total_ref[...] -= product.reshape(9, CAMB, WIDTH)
        return 0

    lax.fori_loop(0, TILES // GROUP, add_group, 0)

    ways = (jnp.where(core == 0, 1, 7), jnp.where(core == 0, 7, 1))
    rings = (ring_a, ring_b)

    def hop(step, ring):
        first, last = SPLIT[ring], SPLIT[ring + 1]
        if step == 0:
            piece = lax.rem(row + 8 - ways[ring], 8)
            source_ref = total_ref.at[first:last, pl.ds(pl.multiple_of(piece * 8, 8), 8), :]
        else:
            source_ref = rings[ring].at[step - 1]
        return pltpu.make_async_remote_copy(
            src_ref=source_ref,
            dst_ref=rings[ring].at[step],
            send_sem=ring_sent.at[ring, step],
            recv_sem=ring_held.at[ring, step],
            device_id=(pt, lax.rem(row + ways[ring], 8), col),
            device_id_type=MESH,
        )

    for ring in range(2):
        hop(0, ring).start()
    for step in range(7):
        for ring in range(2):
            first, last = SPLIT[ring], SPLIT[ring + 1]
            hop(step, ring).wait_recv()
            piece = lax.rem(row + 8 * (step + 2) - (step + 2) * ways[ring], 8)
            mine = total_ref[first:last, pl.ds(pl.multiple_of(piece * 8, 8), 8), :]
            if step < 6:
                rings[ring][step] = rings[ring][step] + mine
                hop(step + 1, ring).start()
            else:
                for parameter in range(first, last):
                    sums = rings[ring][step, parameter - first] + mine[parameter - first]
                    for camera in range(8):
                        goal_row = camera * 9 + parameter
                        rows_ref[goal_row : goal_row + 1, :] = sums[camera : camera + 1]

    stacked = jnp.concatenate(split_three(rows_ref[...]), axis=0)
    ordered = lax.dot_general(stacked, perm_ref[...], NT, preferred_element_type=F32)
    share = ordered[0:72] + ordered[72:144] + ordered[144:216]

    share_ref[...] = share
    upper_copy = pltpu.make_async_remote_copy(
        src_ref=share_ref,
        dst_ref=upper_ref,
        send_sem=share_sem.at[0],
        recv_sem=share_sem.at[1],
        device_id=(row, pt, col),
        device_id_type=MESH,
    )

    @pl.when(same == 0)
    def _():
        upper_copy.start()

    @pl.when(same == 1)
    def _():
        upper_ref[...] = share_ref[...]

    flipped = share.T
    for other in range(8):
        flip_ref[other] = flipped[other * 72 : (other + 1) * 72, :]

    there = lax.rem(pt + 4, 8)

    def flip(other):
        return pltpu.make_async_remote_copy(
            src_ref=flip_ref.at[other],
            dst_ref=blocks_ref.at[row],
            send_sem=flip_sent.at[other],
            recv_sem=flip_held.at[row],
            device_id=(other, there, col),
            device_id_type=MESH,
        )

    def flip_from(other):
        return pltpu.make_async_remote_copy(
            src_ref=flip_ref.at[other],
            dst_ref=blocks_ref.at[other],
            send_sem=flip_sent.at[other],
            recv_sem=flip_held.at[other],
            device_id=(pt, row, col),
            device_id_type=MESH,
        )

    def send_flip(other, _):
        is_self = (other == pt) & (there == row)

        @pl.when(jnp.logical_not(is_self))
        def _():
            flip(other).start()

        @pl.when(is_self)
        def _():
            blocks_ref[row] = flip_ref[other]

        return 0

    lax.fori_loop(0, 8, send_flip, 0)

    for other in range(8):
        @pl.when((mirror != pt) | (row != other))
        def _():
            flip_from(other).wait_recv()

        lower_ref[:, other * 72 : (other + 1) * 72] = blocks_ref[other]

    @pl.when(same == 0)
    def _():
        upper_copy.wait()

    def drain(index, _):
        dispatch(index, (pt, row, col)).wait_send()
        return 0

    lax.fori_loop(1, TILES, drain, 0)
    for step in range(7):
        for ring in range(2):
            hop(step, ring).wait_send()

    def drain_flip(other, _):
        @pl.when((other != pt) | (there != row))
        def _():
            flip(other).wait_send()

        return 0

    lax.fori_loop(0, 8, drain_flip, 0)


def body(jac_cam, jac_pt, obs_cam, point_covisible_tile):
    def rows_of(array):
        observed, _, width, held = array.shape
        array = array.transpose(0, 2, 1, 3).reshape(observed * width, 2, held // LANES, LANES)
        return array.transpose(0, 2, 1, 3).reshape(observed * width * 2 * held // LANES, LANES)

    vmem = pl.BlockSpec(memory_space=pltpu.VMEM)
    upper, lower = pl.pallas_call(
        kernel,
        out_shape=[jax.ShapeDtypeStruct((72, WIDTH), F32)] * 2,
        in_specs=[vmem] * 4,
        out_specs=[vmem] * 2,
        scratch_shapes=[
            pltpu.VMEM((400, 2048), BF16),
            pltpu.VMEM((768, LANES), F32),
            pltpu.VMEM((512, LANES), BF16),
            pltpu.VMEM((16, LANES), F32),
            pltpu.VMEM((256, 2048), BF16),
            pltpu.VMEM((TILES, FEATURES, LANES), F32),
            pltpu.VMEM((TILES, FEATURES, LANES), F32),
            pltpu.VMEM((WIDTH, 3 * LANES * GROUP), BF16),
            pltpu.VMEM((WIDTH, 3 * LANES * GROUP), BF16),
            pltpu.VMEM((9, CAMB, WIDTH), F32),
            pltpu.VMEM((7, 5, 8, WIDTH), F32),
            pltpu.VMEM((7, 4, 8, WIDTH), F32),
            pltpu.VMEM((WIDTH, WIDTH), BF16),
            pltpu.VMEM((72, WIDTH), F32),
            pltpu.VMEM((72, WIDTH), F32),
            pltpu.VMEM((8, 72, 72), F32),
            pltpu.VMEM((8, 72, 72), F32),
            pltpu.SemaphoreType.DMA((TILES,)),
            pltpu.SemaphoreType.DMA((TILES,)),
            pltpu.SemaphoreType.DMA((2, 7)),
            pltpu.SemaphoreType.DMA((2, 7)),
            pltpu.SemaphoreType.DMA((2,)),
            pltpu.SemaphoreType.DMA((8,)),
            pltpu.SemaphoreType.DMA((8,)),
        ],
        compiler_params=pltpu.CompilerParams(
            collective_id=0, has_side_effects=True, vmem_limit_bytes=50 * 2**20
        ),
    )(rows_of(jac_cam), rows_of(jac_pt), obs_cam, point_covisible_tile.reshape(16, LANES))
    return (upper[None], lower[None])


def solution(mesh):
    in_specs = (
        P(None, None, None, ("pt", "row", "col")),
        P(None, None, None, ("pt", "row", "col")),
        P(None, ("pt", "row", "col")),
        P(("pt", "row", "col"), None),
    )
    out_specs = (P(("row", "col"), "pt", None), P(("row", "col"), "pt", None))
    return jax.shard_map(body, mesh=mesh, in_specs=in_specs, out_specs=out_specs, check_vma=False)
```

```python
import functools

import jax
import jax.numpy as jnp
from jax import lax
from jax.experimental import pallas as pl
from jax.experimental.pallas import tpu as pltpu
from jax.sharding import PartitionSpec as P

F32 = jnp.float32
BF16 = jnp.bfloat16
MESH = pl.DeviceIdType.MESH

CAMB = 64
DAMPING = 1.0
LANES = 128
TILES = 32
FEATURES = 200
PT_ROW = 144
CAM_ROW = 192
GROUP = 4
WIDTH = 9 * CAMB
NT = (((1,), (1,)), ((), ()))
CHUNKS = 3
ROWS = 72 // CHUNKS
TWO_HOP = 7


def point_factors(pt_ref, out_ref):
    def entry(obs, coordinate, residual):
        return pt_ref[pl.ds((obs * 3 + coordinate) * 32 + residual, 16, stride=2), :]

    sums = {}
    for first in range(3):
        for second in range(first, 3):
            total = None
            for obs in range(8):
                for residual in range(2):
                    term = entry(obs, first, residual) * entry(obs, second, residual)
                    total = term if total is None else total + term
            sums[first, second] = total + DAMPING if first == second else total
    vzz, vzo, vzt = sums[0, 0], sums[0, 1], sums[0, 2]
    voo, vot, vtt = sums[1, 1], sums[1, 2], sums[2, 2]
    adj_zz = voo * vtt - vot * vot
    adj_zo = vzt * vot - vzo * vtt
    adj_zt = vzo * vot - vzt * voo
    adj_oo = vzz * vtt - vzt * vzt
    adj_ot = vzo * vzt - vzz * vot
    adj_tt = vzz * voo - vzo * vzo
    reciprocal = 1.0 / (vzz * adj_zz + vzo * adj_zo + vzt * adj_zt)
    inverse = [
        [entry_ * reciprocal for entry_ in line]
        for line in ((adj_zz, adj_zo, adj_zt), (adj_zo, adj_oo, adj_ot), (adj_zt, adj_ot, adj_tt))
    ]
    for residual in range(2):
        for obs in range(8):
            parts = [entry(obs, coordinate, residual) for coordinate in range(3)]
            for coordinate in range(3):
                if obs < 4:
                    value = (
                        parts[0] * inverse[0][coordinate]
                        + parts[1] * inverse[1][coordinate]
                        + parts[2] * inverse[2][coordinate]
                    )
                else:
                    value = parts[coordinate]
                row = (residual * 24 + obs * 3 + coordinate) * 16
                out_ref[row : row + 16, :] = value


def ranks(tile_ref, member_ref, rank_ref):
    for block in range(16):
        ids = jnp.broadcast_to(tile_ref[block : block + 1, :], (TILES, LANES))
        same = ids == lax.broadcasted_iota(jnp.int32, (TILES, LANES), 0)
        member_ref[block * TILES : (block + 1) * TILES, :] = jnp.where(same, 1.0, 0.0).astype(BF16)
    rows = lax.broadcasted_iota(jnp.int32, (LANES, LANES), 0)
    columns = lax.broadcasted_iota(jnp.int32, (LANES, LANES), 1)
    earlier = jnp.where(rows < columns, 1.0, 0.0).astype(BF16)
    members = member_ref[...]
    before = jnp.dot(members, earlier, preferred_element_type=F32)
    totals = jnp.dot(members, jnp.ones((LANES, LANES), BF16), preferred_element_type=F32)
    base = jnp.zeros((TILES, LANES), F32)
    for block in range(16):
        span = slice(block * TILES, (block + 1) * TILES)
        own = members[span].astype(F32) * (before[span] + base)
        rank_ref[block : block + 1, :] = jnp.sum(own, axis=0, keepdims=True)
        base = base + totals[span]


def gather_features(cam_ref, factor_ref, obs_ref, x_ref):
    for block in range(16):
        lanes = slice(block * LANES, (block + 1) * LANES)
        parts = [cam_ref[pl.ds(block * 2 + residual, 72, stride=32), :] for residual in range(2)]
        parts.append(factor_ref[pl.ds(block, 48, stride=16), :])
        values = jnp.concatenate(parts, axis=0)
        high = values.astype(BF16)
        x_ref[0:192, lanes] = high
        x_ref[208:400, lanes] = (values - high.astype(F32)).astype(BF16)
        names = obs_ref[:, lanes].astype(F32) + 1.0
        x_ref[192:208, lanes] = jnp.concatenate([names, jnp.zeros((8, LANES), F32)], axis=0).astype(BF16)


def place_points(x_ref, tile_ref, rank_ref, place_ref, wanted):
    slots = lax.broadcasted_iota(jnp.int32, (LANES, LANES), 0).astype(F32).astype(BF16)
    one, zero = jnp.ones((LANES, LANES), BF16), jnp.zeros((LANES, LANES), BF16)
    for part in range(2):
        slot_of = jnp.where(tile_ref[...] == wanted[part], rank_ref[...], -1.0)
        for block in range(16):
            row = jnp.broadcast_to(slot_of[block : block + 1, :], (LANES, LANES)).astype(BF16)
            place_ref[part * LANES : (part + 1) * LANES, block * LANES : (block + 1) * LANES] = jnp.where(
                row == slots, one, zero
            )
    placed = lax.dot_general(x_ref[...], place_ref[...], NT, preferred_element_type=F32)
    return placed[0:192] + placed[208:400], placed[192:200]


def fill_factor(block_ref, half, factor_ref, position):
    labels = (lax.broadcasted_iota(jnp.int32, (CAMB, LANES), 0).astype(F32) + 1.0).astype(BF16)
    cameras, masks, cross = [], [], []
    for index in range(4):
        obs = 4 * half + index
        camera = block_ref[CAM_ROW + obs : CAM_ROW + obs + 1, :]
        cameras.append(camera)
        masks.append(labels == jnp.broadcast_to(camera, (CAMB, LANES)).astype(BF16))
        camera_rows = [block_ref[res * 72 + obs * 9 : res * 72 + obs * 9 + 9, :] for res in range(2)]
        line = []
        for coordinate in range(3):
            rows = [PT_ROW + res * 24 + obs * 3 + coordinate for res in range(2)]
            line.append(
                camera_rows[0] * block_ref[rows[0] : rows[0] + 1, :]
                + camera_rows[1] * block_ref[rows[1] : rows[1] + 1, :]
            )
        cross.append(line)
    for index in range(4):
        for later in range(index + 1, 4):
            same = cameras[index] == cameras[later]
            for coordinate in range(3):
                cross[index][coordinate] = cross[index][coordinate] + jnp.where(same, cross[later][coordinate], 0.0)
    for coordinate in range(3):
        first = (coordinate * GROUP + position) * LANES
        for parameter in range(9):
            value = jnp.zeros((CAMB, LANES), BF16)
            for index in (3, 2, 1, 0):
                row = cross[index][coordinate][parameter : parameter + 1, :]
                value = jnp.where(masks[index], jnp.broadcast_to(row, (CAMB, LANES)).astype(BF16), value)
            factor_ref[parameter * CAMB : (parameter + 1) * CAMB, first : first + LANES] = value


def split_three(value):
    high = value.astype(BF16)
    rest = value - high.astype(F32)
    middle = rest.astype(BF16)
    return high, middle, (rest - middle.astype(F32)).astype(BF16)


def permute_columns(value, perm_ref):
    stacked = jnp.concatenate(split_three(value), axis=0)
    ordered = lax.dot_general(stacked, perm_ref[...], NT, preferred_element_type=F32)
    rows = value.shape[0]
    return ordered[0:rows] + ordered[rows : 2 * rows] + ordered[2 * rows :]


def kernel(
    cam_hbm, pt_hbm, obs_hbm, tile_hbm, upper_ref, lower_ref,
    cam_ref, pt_ref, obs_ref, tile_ref,
    x_ref, factor_ref, member_ref, rank_ref, place_ref, sent_ref, held_ref, relay_ref, left_ref, right_ref,
    total_ref, chain_a, chain_b, perm_ref, piece_ref, row_got, flip_ref, flip_got, lanes_ref,
    load_sem, sent_sem, held_sem, relay_sem, again_sem, chain_sent, chain_held, row_sent, row_held, flip_sent, flip_held,
):
    pt, row, col = lax.axis_index("pt"), lax.axis_index("row"), lax.axis_index("col")
    y, core = pt // 2, lax.rem(pt, 2)

    loads = [
        pltpu.make_async_copy(source, target, load_sem.at[index])
        for index, (source, target) in enumerate(
            ((tile_hbm, tile_ref), (pt_hbm, pt_ref), (obs_hbm, obs_ref), (cam_hbm, cam_ref))
        )
    ]
    for load in loads:
        load.start()

    def device(shift_y, shift_x, part):
        return (lax.rem(y + shift_y, 4) * 2 + (core if part == 0 else 1 - core), row, lax.rem(col + shift_x, 4))

    barrier = pltpu.get_barrier_semaphore()

    def greet(there):
        pl.semaphore_signal(barrier, inc=1, device_id=there, device_id_type=MESH)

    for part in range(2):
        for shift in range(1, 4):
            greet(device(0, shift, part))
            greet(device(shift, 0, part))
    greet(device(0, 0, 1))
    greet((pt, lax.rem(row + 1, 8), col))
    greet((pt, lax.rem(row + 7, 8), col))

    loads[0].wait()
    ranks(tile_ref, member_ref, rank_ref)
    loads[1].wait()
    point_factors(pt_ref, factor_ref)
    loads[2].wait()
    loads[3].wait()
    gather_features(cam_ref, factor_ref, obs_ref, x_ref)

    pl.semaphore_wait(barrier, 15)

    def single(index):
        far, along = index // 2 + 1, lax.rem(index, 2)
        return along * far, (1 - along) * far

    def double(index):
        return lax.rem(index + index // 3, 3) + 1, lax.rem(index, 3) + 1

    def direct(block, there):
        return pltpu.make_async_remote_copy(
            src_ref=sent_ref.at[block],
            dst_ref=held_ref.at[block],
            send_sem=sent_sem.at[block],
            recv_sem=held_sem.at[block],
            device_id=there,
            device_id_type=MESH,
        )

    def first_hop(block, there):
        return pltpu.make_async_remote_copy(
            src_ref=sent_ref.at[block],
            dst_ref=relay_ref.at[block - 2 * TWO_HOP],
            send_sem=sent_sem.at[block],
            recv_sem=relay_sem.at[block - 2 * TWO_HOP],
            device_id=there,
            device_id_type=MESH,
        )

    def second_hop(block, there):
        return pltpu.make_async_remote_copy(
            src_ref=relay_ref.at[block - 2 * TWO_HOP],
            dst_ref=held_ref.at[block],
            send_sem=again_sem.at[block - 2 * TWO_HOP],
            recv_sem=held_sem.at[block],
            device_id=there,
            device_id_type=MESH,
        )

    def place_pair(shift_y, shift_x):
        owners = [device(shift_y, shift_x, part) for part in range(2)]
        wanted = [owner[0] * 4 + owner[2] for owner in owners]
        placed, names = place_points(x_ref, tile_ref, rank_ref, place_ref, wanted)
        return owners, placed, names

    def store(target, block, placed, names, part):
        lanes = slice(part * LANES, (part + 1) * LANES)
        target[block, 0:192, :] = placed[:, lanes]
        target[block, 192:200, :] = names[:, lanes]

    def send_single(index, _):
        owners, placed, names = place_pair(*single(index))
        for part in range(2):
            block = 2 * (index + 1) + part
            store(sent_ref, block, placed, names, part)
            direct(block, owners[part]).start()
        return 0

    def send_double(index, _):
        shift_y, shift_x = double(index)
        _, placed, names = place_pair(shift_y, shift_x)
        block = 2 * (index + TWO_HOP)
        store(sent_ref, block, placed, names, 0)
        first_hop(block, device(0, shift_x, 0)).start()
        store(sent_ref, block + 1, placed, names, 1)
        first_hop(block + 1, device(shift_y, 0, 0)).start()
        return 0

    lax.fori_loop(0, 6, send_single, 0)
    lax.fori_loop(0, 9, send_double, 0)
    owners, placed, names = place_pair(0, 0)
    store(held_ref, 0, placed, names, 0)
    store(sent_ref, 1, placed, names, 1)
    direct(1, owners[1]).start()

    source = lax.broadcasted_iota(jnp.int32, (WIDTH, WIDTH), 1)
    goal = lax.broadcasted_iota(jnp.int32, (WIDTH, WIDTH), 0)
    perm_ref[...] = jnp.where((source & 63) * 9 + (source >> 6) == goal, 1.0, 0.0).astype(BF16)
    piece_ref[72:128, :] = jnp.zeros((56, WIDTH), F32)
    total_ref[...] = jnp.zeros_like(total_ref)

    def forward(index, _):
        shift_y, shift_x = double(index)
        block = 2 * (index + TWO_HOP)
        first_hop(block, (pt, row, col)).wait_recv()
        second_hop(block, device(shift_y, 0, 0)).start()
        first_hop(block + 1, (pt, row, col)).wait_recv()
        second_hop(block + 1, device(0, shift_x, 1)).start()
        return 0

    def add_group(group, _):
        start = jnp.where(group >= 5, 9, jnp.maximum(2 * group - 2, 0))
        stop = jnp.where(group >= 4, 9, 2 * group)
        lax.fori_loop(start, stop, forward, 0)
        for position in range(GROUP):
            index = group * GROUP + position

            @pl.when(index > 0)
            def _():
                direct(index, (pt, row, col)).wait_recv()

        for position in range(GROUP):
            block = held_ref.at[group * GROUP + position]
            fill_factor(block, 0, left_ref, position)
            fill_factor(block, 1, right_ref, position)
        product = lax.dot_general(left_ref[...], right_ref[...], NT, preferred_element_type=F32)
        total_ref[:, 0:64, :] -= product[0:512].reshape(8, 64, WIDTH)
        total_ref[:, 64:72, :] -= product[512:576].reshape(8, 8, WIDTH)
        return 0

    lax.fori_loop(0, TILES // GROUP, add_group, 0)

    ways = (jnp.where(core == 0, 1, 7), jnp.where(core == 0, 7, 1))
    chains = (chain_a, chain_b)
    hops = (4, 3)

    def piece_at(side, distance):
        return lax.rem(row + distance * ways[side], 8)

    def hop(side, step, chunk):
        span = slice(chunk * ROWS, (chunk + 1) * ROWS)
        source_ref = total_ref.at[piece_at(side, hops[side]), span] if step == 0 else chains[side].at[step - 1, span]
        return pltpu.make_async_remote_copy(
            src_ref=source_ref,
            dst_ref=chains[side].at[step, span],
            send_sem=chain_sent.at[side, step, chunk],
            recv_sem=chain_held.at[side, step, chunk],
            device_id=(pt, piece_at(side, 1), col),
            device_id_type=MESH,
        )

    there = lax.rem(pt + 4, 8)
    mirror = lax.rem(row + 4, 8)

    def send_row(other):
        return pltpu.make_async_remote_copy(
            src_ref=piece_ref.at[pl.ds(pl.multiple_of(other * 8, 8), 8), :],
            dst_ref=row_got.at[row],
            send_sem=row_sent.at[other],
            recv_sem=row_held.at[row],
            device_id=(other, pt, col),
            device_id_type=MESH,
        )

    def take_row(other):
        return pltpu.make_async_remote_copy(
            src_ref=piece_ref.at[pl.ds(pl.multiple_of(other * 8, 8), 8), :],
            dst_ref=row_got.at[other],
            send_sem=row_sent.at[other],
            recv_sem=row_held.at[other],
            device_id=(pt, row, col),
            device_id_type=MESH,
        )

    last_row = pltpu.make_async_remote_copy(
        src_ref=piece_ref.at[64:72, :],
        dst_ref=row_got.at[8],
        send_sem=row_sent.at[8],
        recv_sem=row_held.at[8],
        device_id=(row, pt, col),
        device_id_type=MESH,
    )

    def send_flip(other):
        return pltpu.make_async_remote_copy(
            src_ref=flip_ref.at[other],
            dst_ref=flip_got.at[row],
            send_sem=flip_sent.at[other],
            recv_sem=flip_held.at[row],
            device_id=(other, there, col),
            device_id_type=MESH,
        )

    def take_flip(other):
        return pltpu.make_async_remote_copy(
            src_ref=flip_ref.at[other],
            dst_ref=flip_got.at[other],
            send_sem=flip_sent.at[other],
            recv_sem=flip_held.at[other],
            device_id=(pt, row, col),
            device_id_type=MESH,
        )

    def start_row(other, _):
        is_self = (other == pt) & (pt == row)

        @pl.when(jnp.logical_not(is_self))
        def _():
            send_row(other).start()

        @pl.when(is_self)
        def _():
            row_got[row] = piece_ref[pl.ds(pl.multiple_of(other * 8, 8), 8), :]

        return 0

    def start_flip(index, _):
        other = lax.rem(pt + index, 8)
        is_self = (other == pt) & (there == row)

        @pl.when(jnp.logical_not(is_self))
        def _():
            send_flip(other).start()

        @pl.when(is_self)
        def _():
            flip_got[row] = flip_ref[other]

        return 0

    for chunk in range(CHUNKS):
        for side in range(2):
            hop(side, 0, chunk).start()
    for step in range(3):
        for chunk in range(CHUNKS):
            span = slice(chunk * ROWS, (chunk + 1) * ROWS)
            for side in range(2):
                if step < hops[side] - 1:
                    hop(side, step, chunk).wait_recv()
                    mine = total_ref[piece_at(side, hops[side] - 1 - step), span, :]
                    chains[side][step, span, :] = chains[side][step, span, :] + mine
                    hop(side, step + 1, chunk).start()
    for chunk in range(CHUNKS):
        span = slice(chunk * ROWS, (chunk + 1) * ROWS)
        hop(1, 2, chunk).wait_recv()
        hop(0, 3, chunk).wait_recv()
        piece_ref[span, :] = chain_a[3, span, :] + chain_b[2, span, :] + total_ref[row, span, :]
        lax.fori_loop(chunk * ROWS // 8, min((chunk + 1) * ROWS // 8, 8), start_row, 0)

    @pl.when(pt != row)
    def _():
        last_row.start()

    @pl.when(pt == row)
    def _():
        row_got[8] = piece_ref[64:72, :]

    flipped = piece_ref[...].T
    for other in range(8):
        for parameter in range(9):
            first = parameter * CAMB + other * 8
            flip_ref[other, parameter] = flipped[first : first + 8, :]
    lax.fori_loop(0, 8, start_flip, 0)

    def write_rows(target_ref, value):
        for parameter in range(9):
            for camera in range(8):
                goal_row, source_row = camera * 9 + parameter, parameter * 8 + camera
                target_ref[goal_row : goal_row + 1, :] = value[source_row : source_row + 1]

    for other in range(8):
        @pl.when((pt != row) | (row != other))
        def _():
            take_row(other).wait_recv()

    @pl.when(pt != row)
    def _():
        last_row.wait_recv()

    write_rows(upper_ref, permute_columns(row_got[...].reshape(72, WIDTH), perm_ref))

    for other in range(8):
        @pl.when((mirror != pt) | (row != other))
        def _():
            take_flip(other).wait_recv()

        block = flip_got[other].reshape(72, LANES)
        lanes_ref[:, other * 64 : (other + 1) * 64] = block[:, 0:64]
        lanes_ref[:, 512 + other * 8 : 520 + other * 8] = block[:, 64:72]
    write_rows(lower_ref, permute_columns(lanes_ref[...], perm_ref))

    def drain(block, _):
        direct(block, (pt, row, col)).wait_send()
        return 0

    def drain_again(block, _):
        second_hop(block, (pt, row, col)).wait_send()
        return 0

    lax.fori_loop(1, TILES, drain, 0)
    lax.fori_loop(2 * TWO_HOP, TILES, drain_again, 0)
    for side in range(2):
        for step in range(hops[side]):
            for chunk in range(CHUNKS):
                hop(side, step, chunk).wait_send()

    @pl.when(pt != row)
    def _():
        last_row.wait_send()

    def drain_blocks(other, _):
        @pl.when((other != pt) | (pt != row))
        def _():
            send_row(other).wait_send()

        @pl.when((other != pt) | (there != row))
        def _():
            send_flip(other).wait_send()

        return 0

    lax.fori_loop(0, 8, drain_blocks, 0)


def body(jac_cam, jac_pt, obs_cam, point_covisible_tile):
    def rows_of(array):
        observed, _, width, held = array.shape
        array = array.transpose(0, 2, 1, 3).reshape(observed * width, 2, held // LANES, LANES)
        return array.transpose(0, 2, 1, 3).reshape(observed * width * 2 * held // LANES, LANES)

    vmem = pl.BlockSpec(memory_space=pltpu.VMEM)
    upper, lower = pl.pallas_call(
        kernel,
        out_shape=[jax.ShapeDtypeStruct((72, WIDTH), F32)] * 2,
        in_specs=[pl.BlockSpec(memory_space=pl.ANY)] * 4,
        out_specs=[vmem] * 2,
        scratch_shapes=[
            pltpu.VMEM((2304, LANES), F32),
            pltpu.VMEM((768, LANES), F32),
            pltpu.VMEM((8, 2048), jnp.int32),
            pltpu.VMEM((16, LANES), jnp.int32),
            pltpu.VMEM((400, 2048), BF16),
            pltpu.VMEM((768, LANES), F32),
            pltpu.VMEM((512, LANES), BF16),
            pltpu.VMEM((16, LANES), F32),
            pltpu.VMEM((256, 2048), BF16),
            pltpu.VMEM((TILES, FEATURES, LANES), F32),
            pltpu.VMEM((TILES, FEATURES, LANES), F32),
            pltpu.VMEM((18, FEATURES, LANES), F32),
            pltpu.VMEM((WIDTH, 3 * LANES * GROUP), BF16),
            pltpu.VMEM((WIDTH, 3 * LANES * GROUP), BF16),
            pltpu.VMEM((8, 72, WIDTH), F32),
            pltpu.VMEM((4, 72, WIDTH), F32),
            pltpu.VMEM((3, 72, WIDTH), F32),
            pltpu.VMEM((WIDTH, WIDTH), BF16),
            pltpu.VMEM((LANES, WIDTH), F32),
            pltpu.VMEM((9, 8, WIDTH), F32),
            pltpu.VMEM((8, 9, 8, LANES), F32),
            pltpu.VMEM((8, 9, 8, LANES), F32),
            pltpu.VMEM((72, WIDTH), F32),
            pltpu.SemaphoreType.DMA((4,)),
            pltpu.SemaphoreType.DMA((TILES,)),
            pltpu.SemaphoreType.DMA((TILES,)),
            pltpu.SemaphoreType.DMA((18,)),
            pltpu.SemaphoreType.DMA((18,)),
            pltpu.SemaphoreType.DMA((2, 4, CHUNKS)),
            pltpu.SemaphoreType.DMA((2, 4, CHUNKS)),
            pltpu.SemaphoreType.DMA((9,)),
            pltpu.SemaphoreType.DMA((9,)),
            pltpu.SemaphoreType.DMA((8,)),
            pltpu.SemaphoreType.DMA((8,)),
        ],
        compiler_params=pltpu.CompilerParams(
            collective_id=0, has_side_effects=True, vmem_limit_bytes=50 * 2**20
        ),
    )(rows_of(jac_cam), rows_of(jac_pt), obs_cam, point_covisible_tile.reshape(16, LANES))
    return (upper[None], lower[None])


def solution(mesh):
    in_specs = (
        P(None, None, None, ("pt", "row", "col")),
        P(None, None, None, ("pt", "row", "col")),
        P(None, ("pt", "row", "col")),
        P(("pt", "row", "col"), None),
    )
    out_specs = (P(("row", "col"), "pt", None), P(("row", "col"), "pt", None))
    return jax.shard_map(body, mesh=mesh, in_specs=in_specs, out_specs=out_specs, check_vma=False)
```

```python
import functools

import jax
import jax.numpy as jnp
from jax import lax
from jax.experimental import pallas as pl
from jax.experimental.pallas import tpu as pltpu
from jax.sharding import PartitionSpec as P

F32 = jnp.float32
BF16 = jnp.bfloat16
MESH = pl.DeviceIdType.MESH

CAMB = 64
DAMPING = 1.0
LANES = 128
TILES = 32
FEATURES = 200
PT_ROW = 144
CAM_ROW = 192
GROUP = 2
WIDTH = 9 * CAMB
NT = (((1,), (1,)), ((), ()))
CHUNKS = 3
ROWS = 72 // CHUNKS
TWO_HOP = 7


def point_factors(pt_ref, out_ref):
    def entry(obs, coordinate, residual):
        return pt_ref[pl.ds((obs * 3 + coordinate) * 32 + residual, 16, stride=2), :]

    sums = {}
    for first in range(3):
        for second in range(first, 3):
            total = None
            for obs in range(8):
                for residual in range(2):
                    term = entry(obs, first, residual) * entry(obs, second, residual)
                    total = term if total is None else total + term
            sums[first, second] = total + DAMPING if first == second else total
    vzz, vzo, vzt = sums[0, 0], sums[0, 1], sums[0, 2]
    voo, vot, vtt = sums[1, 1], sums[1, 2], sums[2, 2]
    adj_zz = voo * vtt - vot * vot
    adj_zo = vzt * vot - vzo * vtt
    adj_zt = vzo * vot - vzt * voo
    adj_oo = vzz * vtt - vzt * vzt
    adj_ot = vzo * vzt - vzz * vot
    adj_tt = vzz * voo - vzo * vzo
    reciprocal = 1.0 / (vzz * adj_zz + vzo * adj_zo + vzt * adj_zt)
    inverse = [
        [entry_ * reciprocal for entry_ in line]
        for line in ((adj_zz, adj_zo, adj_zt), (adj_zo, adj_oo, adj_ot), (adj_zt, adj_ot, adj_tt))
    ]
    for residual in range(2):
        for obs in range(8):
            parts = [entry(obs, coordinate, residual) for coordinate in range(3)]
            for coordinate in range(3):
                if obs < 4:
                    value = (
                        parts[0] * inverse[0][coordinate]
                        + parts[1] * inverse[1][coordinate]
                        + parts[2] * inverse[2][coordinate]
                    )
                else:
                    value = parts[coordinate]
                row = (residual * 24 + obs * 3 + coordinate) * 16
                out_ref[row : row + 16, :] = value


def ranks(tile_ref, member_ref, rank_ref):
    for block in range(16):
        ids = jnp.broadcast_to(tile_ref[block : block + 1, :], (TILES, LANES))
        same = ids == lax.broadcasted_iota(jnp.int32, (TILES, LANES), 0)
        member_ref[block * TILES : (block + 1) * TILES, :] = jnp.where(same, 1.0, 0.0).astype(BF16)
    rows = lax.broadcasted_iota(jnp.int32, (LANES, LANES), 0)
    columns = lax.broadcasted_iota(jnp.int32, (LANES, LANES), 1)
    earlier = jnp.where(rows < columns, 1.0, 0.0).astype(BF16)
    members = member_ref[...]
    before = jnp.dot(members, earlier, preferred_element_type=F32)
    totals = jnp.dot(members, jnp.ones((LANES, LANES), BF16), preferred_element_type=F32)
    base = jnp.zeros((TILES, LANES), F32)
    for block in range(16):
        span = slice(block * TILES, (block + 1) * TILES)
        own = members[span].astype(F32) * (before[span] + base)
        rank_ref[block : block + 1, :] = jnp.sum(own, axis=0, keepdims=True)
        base = base + totals[span]


def gather_features(cam_ref, factor_ref, obs_ref, x_ref):
    for block in range(16):
        lanes = slice(block * LANES, (block + 1) * LANES)
        parts = [cam_ref[pl.ds(block * 2 + residual, 72, stride=32), :] for residual in range(2)]
        parts.append(factor_ref[pl.ds(block, 48, stride=16), :])
        values = jnp.concatenate(parts, axis=0)
        high = values.astype(BF16)
        x_ref[0:192, lanes] = high
        x_ref[208:400, lanes] = (values - high.astype(F32)).astype(BF16)
        names = obs_ref[:, lanes].astype(F32) + 1.0
        x_ref[192:208, lanes] = jnp.concatenate([names, jnp.zeros((8, LANES), F32)], axis=0).astype(BF16)


def place_points(x_ref, tile_ref, rank_ref, place_ref, wanted):
    slots = lax.broadcasted_iota(jnp.int32, (LANES, LANES), 0).astype(F32).astype(BF16)
    one, zero = jnp.ones((LANES, LANES), BF16), jnp.zeros((LANES, LANES), BF16)
    for part in range(2):
        slot_of = jnp.where(tile_ref[...] == wanted[part], rank_ref[...], -1.0)
        for block in range(16):
            row = jnp.broadcast_to(slot_of[block : block + 1, :], (LANES, LANES)).astype(BF16)
            place_ref[part * LANES : (part + 1) * LANES, block * LANES : (block + 1) * LANES] = jnp.where(
                row == slots, one, zero
            )
    placed = lax.dot_general(x_ref[...], place_ref[...], NT, preferred_element_type=F32)
    return placed[0:192] + placed[208:400], placed[192:200]


def fill_factor(block_ref, half, factor_ref, position):
    labels = (lax.broadcasted_iota(jnp.int32, (CAMB, LANES), 0).astype(F32) + 1.0).astype(BF16)
    cameras, masks, cross = [], [], []
    for index in range(4):
        obs = 4 * half + index
        camera = block_ref[CAM_ROW + obs : CAM_ROW + obs + 1, :]
        cameras.append(camera)
        masks.append(labels == jnp.broadcast_to(camera, (CAMB, LANES)).astype(BF16))
        camera_rows = [block_ref[res * 72 + obs * 9 : res * 72 + obs * 9 + 9, :] for res in range(2)]
        line = []
        for coordinate in range(3):
            rows = [PT_ROW + res * 24 + obs * 3 + coordinate for res in range(2)]
            line.append(
                camera_rows[0] * block_ref[rows[0] : rows[0] + 1, :]
                + camera_rows[1] * block_ref[rows[1] : rows[1] + 1, :]
            )
        cross.append(line)
    for index in range(4):
        for later in range(index + 1, 4):
            same = cameras[index] == cameras[later]
            for coordinate in range(3):
                cross[index][coordinate] = cross[index][coordinate] + jnp.where(same, cross[later][coordinate], 0.0)
    for coordinate in range(3):
        first = (coordinate * GROUP + position) * LANES
        for parameter in range(9):
            value = jnp.zeros((CAMB, LANES), BF16)
            for index in (3, 2, 1, 0):
                row = cross[index][coordinate][parameter : parameter + 1, :]
                value = jnp.where(masks[index], jnp.broadcast_to(row, (CAMB, LANES)).astype(BF16), value)
            factor_ref[parameter * CAMB : (parameter + 1) * CAMB, first : first + LANES] = value


def split_three(value):
    high = value.astype(BF16)
    rest = value - high.astype(F32)
    middle = rest.astype(BF16)
    return high, middle, (rest - middle.astype(F32)).astype(BF16)


def permute_columns(value, perm_ref):
    stacked = jnp.concatenate(split_three(value), axis=0)
    ordered = lax.dot_general(stacked, perm_ref[...], NT, preferred_element_type=F32)
    rows = value.shape[0]
    return ordered[0:rows] + ordered[rows : 2 * rows] + ordered[2 * rows :]


def kernel(
    cam_hbm, pt_hbm, obs_hbm, tile_hbm, upper_ref, lower_ref,
    cam_ref, pt_ref, obs_ref, tile_ref,
    x_ref, factor_ref, member_ref, rank_ref, place_ref, sent_ref, held_ref, relay_ref, left_ref, right_ref,
    total_ref, chain_a, chain_b, perm_ref, piece_ref, folded_ref, row_mid, row_got, flip_ref, flip_mid, flip_got, lanes_ref,
    load_sem, sent_sem, held_sem, relay_sem, again_sem, chain_sent, chain_held, mid_sent, mid_held, end_sent, end_held, last_sem,
):
    pt, row, col = lax.axis_index("pt"), lax.axis_index("row"), lax.axis_index("col")
    y, core = pt // 2, lax.rem(pt, 2)

    loads = [
        pltpu.make_async_copy(source, target, load_sem.at[index])
        for index, (source, target) in enumerate(
            ((tile_hbm, tile_ref), (pt_hbm, pt_ref), (obs_hbm, obs_ref), (cam_hbm, cam_ref))
        )
    ]
    for load in loads:
        load.start()

    def device(shift_y, shift_x, part):
        return (lax.rem(y + shift_y, 4) * 2 + (core if part == 0 else 1 - core), row, lax.rem(col + shift_x, 4))

    barrier = pltpu.get_barrier_semaphore()

    def greet(there):
        pl.semaphore_signal(barrier, inc=1, device_id=there, device_id_type=MESH)

    for part in range(2):
        for shift in range(1, 4):
            greet(device(0, shift, part))
            greet(device(shift, 0, part))
    greet(device(0, 0, 1))
    greet((pt, lax.rem(row + 1, 8), col))
    greet((pt, lax.rem(row + 7, 8), col))

    loads[0].wait()
    ranks(tile_ref, member_ref, rank_ref)
    loads[1].wait()
    point_factors(pt_ref, factor_ref)
    loads[2].wait()
    loads[3].wait()
    gather_features(cam_ref, factor_ref, obs_ref, x_ref)

    pl.semaphore_wait(barrier, 15)

    def single(index):
        far, along = index // 2 + 1, lax.rem(index, 2)
        return along * far, (1 - along) * far

    def double(index):
        return lax.rem(index + index // 3, 3) + 1, lax.rem(index, 3) + 1

    def direct(block, there):
        return pltpu.make_async_remote_copy(
            src_ref=sent_ref.at[block],
            dst_ref=held_ref.at[block],
            send_sem=sent_sem.at[block],
            recv_sem=held_sem.at[block],
            device_id=there,
            device_id_type=MESH,
        )

    def first_hop(block, there):
        return pltpu.make_async_remote_copy(
            src_ref=sent_ref.at[block],
            dst_ref=relay_ref.at[block - 2 * TWO_HOP],
            send_sem=sent_sem.at[block],
            recv_sem=relay_sem.at[block - 2 * TWO_HOP],
            device_id=there,
            device_id_type=MESH,
        )

    def second_hop(block, there):
        return pltpu.make_async_remote_copy(
            src_ref=relay_ref.at[block - 2 * TWO_HOP],
            dst_ref=held_ref.at[block],
            send_sem=again_sem.at[block - 2 * TWO_HOP],
            recv_sem=held_sem.at[block],
            device_id=there,
            device_id_type=MESH,
        )

    def place_pair(shift_y, shift_x):
        owners = [device(shift_y, shift_x, part) for part in range(2)]
        wanted = [owner[0] * 4 + owner[2] for owner in owners]
        placed, names = place_points(x_ref, tile_ref, rank_ref, place_ref, wanted)
        return owners, placed, names

    def store(target, block, placed, names, part):
        lanes = slice(part * LANES, (part + 1) * LANES)
        target[block, 0:192, :] = placed[:, lanes]
        target[block, 192:200, :] = names[:, lanes]

    def send_single(index, _):
        owners, placed, names = place_pair(*single(index))
        for part in range(2):
            block = 2 * (index + 1) + part
            store(sent_ref, block, placed, names, part)
            direct(block, owners[part]).start()
        return 0

    def send_double(index, _):
        shift_y, shift_x = double(index)
        _, placed, names = place_pair(shift_y, shift_x)
        block = 2 * (index + TWO_HOP)
        store(sent_ref, block, placed, names, 0)
        first_hop(block, device(0, shift_x, 0)).start()
        store(sent_ref, block + 1, placed, names, 1)
        first_hop(block + 1, device(shift_y, 0, 0)).start()
        return 0

    lax.fori_loop(0, 6, send_single, 0)
    lax.fori_loop(0, 9, send_double, 0)
    owners, placed, names = place_pair(0, 0)
    store(held_ref, 0, placed, names, 0)
    store(sent_ref, 1, placed, names, 1)
    direct(1, owners[1]).start()

    source = lax.broadcasted_iota(jnp.int32, (WIDTH, WIDTH), 1)
    goal = lax.broadcasted_iota(jnp.int32, (WIDTH, WIDTH), 0)
    perm_ref[...] = jnp.where((source & 63) * 9 + (source >> 6) == goal, 1.0, 0.0).astype(BF16)
    folded_ref[...] = jnp.zeros_like(folded_ref)
    total_ref[...] = jnp.zeros_like(total_ref)

    def forward(index, _):
        shift_y, shift_x = double(index)
        block = 2 * (index + TWO_HOP)
        first_hop(block, (pt, row, col)).wait_recv()
        second_hop(block, device(shift_y, 0, 0)).start()
        first_hop(block + 1, (pt, row, col)).wait_recv()
        second_hop(block + 1, device(0, shift_x, 1)).start()
        return 0

    def add_group(group, _):
        start = jnp.where(group >= 9, 9, jnp.maximum(group - 1, 0))
        stop = jnp.where(group >= 8, 9, group)
        lax.fori_loop(start, stop, forward, 0)
        for position in range(GROUP):
            index = group * GROUP + position

            @pl.when(index > 0)
            def _():
                direct(index, (pt, row, col)).wait_recv()

        for position in range(GROUP):
            block = held_ref.at[group * GROUP + position]
            fill_factor(block, 0, left_ref, position)
            fill_factor(block, 1, right_ref, position)
        product = lax.dot_general(left_ref[...], right_ref[...], NT, preferred_element_type=F32)
        total_ref[:, 0:64, :] -= product[0:512].reshape(8, 64, WIDTH)
        total_ref[:, 64:72, :] -= product[512:576].reshape(8, 8, WIDTH)
        return 0

    lax.fori_loop(0, TILES // GROUP, add_group, 0)

    ways = (jnp.where(core == 0, 1, 7), jnp.where(core == 0, 7, 1))
    chains = (chain_a, chain_b)
    hops = (4, 3)

    def piece_at(side, distance):
        return lax.rem(row + distance * ways[side], 8)

    def hop(side, step, chunk):
        span = slice(chunk * ROWS, (chunk + 1) * ROWS)
        source_ref = total_ref.at[piece_at(side, hops[side]), span] if step == 0 else chains[side].at[step - 1, span]
        return pltpu.make_async_remote_copy(
            src_ref=source_ref,
            dst_ref=chains[side].at[step, span],
            send_sem=chain_sent.at[side, step, chunk],
            recv_sem=chain_held.at[side, step, chunk],
            device_id=(pt, piece_at(side, 1), col),
            device_id_type=MESH,
        )

    mirror = lax.rem(row + 4, 8)
    middles = (row_mid, flip_mid)
    ends = (row_got, flip_got)

    def block_of(kind, other):
        if kind == 1:
            return flip_ref.at[other]
        return piece_ref.at[pl.ds(pl.multiple_of(other * 8, 8), 8), :]

    def to_middle(kind, other, slot):
        return pltpu.make_async_remote_copy(
            src_ref=block_of(kind, other),
            dst_ref=middles[kind].at[slot],
            send_sem=mid_sent.at[kind, other],
            recv_sem=mid_held.at[kind, slot],
            device_id=(other, row, col),
            device_id_type=MESH,
        )

    def to_end(kind, other, slot):
        return pltpu.make_async_remote_copy(
            src_ref=middles[kind].at[other],
            dst_ref=ends[kind].at[slot],
            send_sem=end_sent.at[kind, other],
            recv_sem=end_held.at[kind, slot],
            device_id=(pt, other if kind == 0 else lax.rem(other + 4, 8), col),
            device_id_type=MESH,
        )

    last_row = pltpu.make_async_remote_copy(
        src_ref=piece_ref.at[64:72, :],
        dst_ref=row_got.at[8],
        send_sem=last_sem.at[0],
        recv_sem=last_sem.at[1],
        device_id=(row, pt, col),
        device_id_type=MESH,
    )

    def start_middle(kind, first, last):
        def start(other, _):
            @pl.when(other != pt)
            def _():
                to_middle(kind, other, pt).start()

            @pl.when(other == pt)
            def _():
                middles[kind][other] = block_of(kind, other)[...]

            return 0

        lax.fori_loop(first, last, start, 0)

    def start_end(kind):
        own = row if kind == 0 else mirror

        def start(index, _):
            other = lax.rem(pt + index, 8)

            @pl.when(other != pt)
            def _():
                to_middle(kind, other, other).wait_recv()

            @pl.when(other != own)
            def _():
                to_end(kind, other, row).start()

            @pl.when(other == own)
            def _():
                ends[kind][row] = middles[kind][other]

            return 0

        lax.fori_loop(0, 8, start, 0)

    for chunk in range(CHUNKS):
        for side in range(2):
            hop(side, 0, chunk).start()
    for step in range(3):
        for chunk in range(CHUNKS):
            span = slice(chunk * ROWS, (chunk + 1) * ROWS)
            for side in range(2):
                if step < hops[side] - 1:
                    hop(side, step, chunk).wait_recv()
                    mine = total_ref[piece_at(side, hops[side] - 1 - step), span, :]
                    chains[side][step, span, :] = chains[side][step, span, :] + mine
                    hop(side, step + 1, chunk).start()
    for chunk in range(CHUNKS):
        span = slice(chunk * ROWS, (chunk + 1) * ROWS)
        hop(1, 2, chunk).wait_recv()
        hop(0, 3, chunk).wait_recv()
        piece_ref[span, :] = chain_a[3, span, :] + chain_b[2, span, :] + total_ref[row, span, :]
        start_middle(0, chunk * ROWS // 8, min((chunk + 1) * ROWS // 8, 8))

    @pl.when(pt != row)
    def _():
        last_row.start()

    @pl.when(pt == row)
    def _():
        row_got[8] = piece_ref[64:72, :]

    folded_ref[0:64, 0:256] = piece_ref[0:64, 0:256]
    folded_ref[64:128, 0:256] = piece_ref[0:64, 256:512]
    folded_ref[0:64, 256:320] = piece_ref[0:64, 512:576]
    for parameter in range(8):
        folded_ref[64 + parameter * 8 : 72 + parameter * 8, 256:320] = piece_ref[
            64:72, parameter * 64 : (parameter + 1) * 64
        ]
    folded_ref[0:8, 320:384] = piece_ref[64:72, 512:576]
    flipped = folded_ref[...].T
    for other in range(8):
        for tile in range(6):
            first = tile * CAMB + other * 8
            flip_ref[other, tile] = flipped[first : first + 8, :]
    start_middle(1, 0, 8)
    start_end(0)
    start_end(1)

    def write_rows(target_ref, value):
        for parameter in range(9):
            for camera in range(8):
                goal_row, source_row = camera * 9 + parameter, parameter * 8 + camera
                target_ref[goal_row : goal_row + 1, :] = value[source_row : source_row + 1]

    for other in range(8):
        @pl.when(row != other)
        def _():
            to_end(0, other, other).wait_recv()

    @pl.when(pt != row)
    def _():
        last_row.wait_recv()

    write_rows(upper_ref, permute_columns(row_got[...].reshape(72, WIDTH), perm_ref))

    for other in range(8):
        @pl.when(row != other)
        def _():
            to_end(1, other, other).wait_recv()

        for parameter in range(9):
            rows = slice(parameter * 8, (parameter + 1) * 8)
            tile, lane = (4, 0) if parameter == 8 else (parameter % 4, parameter // 4 * 64)
            lanes_ref[rows, other * 64 : (other + 1) * 64] = flip_got[other, tile, :, lane : lane + 64]
            tile, lane = (5, 0) if parameter == 8 else (4, 64 + parameter * 8)
            lanes_ref[rows, 512 + other * 8 : 520 + other * 8] = flip_got[other, tile, :, lane : lane + 8]
    write_rows(lower_ref, permute_columns(lanes_ref[...], perm_ref))

    def drain(block, _):
        direct(block, (pt, row, col)).wait_send()
        return 0

    def drain_again(block, _):
        second_hop(block, (pt, row, col)).wait_send()
        return 0

    lax.fori_loop(1, TILES, drain, 0)
    lax.fori_loop(2 * TWO_HOP, TILES, drain_again, 0)
    for side in range(2):
        for step in range(hops[side]):
            for chunk in range(CHUNKS):
                hop(side, step, chunk).wait_send()

    @pl.when(pt != row)
    def _():
        last_row.wait_send()

    def drain_blocks(other, _):
        for kind in range(2):

            @pl.when(other != pt)
            def _(kind=kind):
                to_middle(kind, other, pt).wait_send()

            @pl.when(other != (row if kind == 0 else mirror))
            def _(kind=kind):
                to_end(kind, other, row).wait_send()

        return 0

    lax.fori_loop(0, 8, drain_blocks, 0)


def body(jac_cam, jac_pt, obs_cam, point_covisible_tile):
    def rows_of(array):
        observed, _, width, held = array.shape
        array = array.transpose(0, 2, 1, 3).reshape(observed * width, 2, held // LANES, LANES)
        return array.transpose(0, 2, 1, 3).reshape(observed * width * 2 * held // LANES, LANES)

    vmem = pl.BlockSpec(memory_space=pltpu.VMEM)
    upper, lower = pl.pallas_call(
        kernel,
        out_shape=[jax.ShapeDtypeStruct((72, WIDTH), F32)] * 2,
        in_specs=[pl.BlockSpec(memory_space=pl.ANY)] * 4,
        out_specs=[vmem] * 2,
        scratch_shapes=[
            pltpu.VMEM((2304, LANES), F32),
            pltpu.VMEM((768, LANES), F32),
            pltpu.VMEM((8, 2048), jnp.int32),
            pltpu.VMEM((16, LANES), jnp.int32),
            pltpu.VMEM((400, 2048), BF16),
            pltpu.VMEM((768, LANES), F32),
            pltpu.VMEM((512, LANES), BF16),
            pltpu.VMEM((16, LANES), F32),
            pltpu.VMEM((256, 2048), BF16),
            pltpu.VMEM((TILES, FEATURES, LANES), F32),
            pltpu.VMEM((TILES, FEATURES, LANES), F32),
            pltpu.VMEM((18, FEATURES, LANES), F32),
            pltpu.VMEM((WIDTH, 3 * LANES * GROUP), BF16),
            pltpu.VMEM((WIDTH, 3 * LANES * GROUP), BF16),
            pltpu.VMEM((8, 72, WIDTH), F32),
            pltpu.VMEM((4, 72, WIDTH), F32),
            pltpu.VMEM((3, 72, WIDTH), F32),
            pltpu.VMEM((WIDTH, WIDTH), BF16),
            pltpu.VMEM((72, WIDTH), F32),
            pltpu.VMEM((LANES, 384), F32),
            pltpu.VMEM((8, 8, WIDTH), F32),
            pltpu.VMEM((9, 8, WIDTH), F32),
            pltpu.VMEM((8, 6, 8, LANES), F32),
            pltpu.VMEM((8, 6, 8, LANES), F32),
            pltpu.VMEM((8, 6, 8, LANES), F32),
            pltpu.VMEM((72, WIDTH), F32),
            pltpu.SemaphoreType.DMA((4,)),
            pltpu.SemaphoreType.DMA((TILES,)),
            pltpu.SemaphoreType.DMA((TILES,)),
            pltpu.SemaphoreType.DMA((18,)),
            pltpu.SemaphoreType.DMA((18,)),
            pltpu.SemaphoreType.DMA((2, 4, CHUNKS)),
            pltpu.SemaphoreType.DMA((2, 4, CHUNKS)),
            pltpu.SemaphoreType.DMA((2, 8)),
            pltpu.SemaphoreType.DMA((2, 8)),
            pltpu.SemaphoreType.DMA((2, 8)),
            pltpu.SemaphoreType.DMA((2, 8)),
            pltpu.SemaphoreType.DMA((2,)),
        ],
        compiler_params=pltpu.CompilerParams(
            collective_id=0, has_side_effects=True, vmem_limit_bytes=64 * 2**20 - 2**19
        ),
    )(rows_of(jac_cam), rows_of(jac_pt), obs_cam, point_covisible_tile.reshape(16, LANES))
    return (upper[None], lower[None])


def solution(mesh):
    in_specs = (
        P(None, None, None, ("pt", "row", "col")),
        P(None, None, None, ("pt", "row", "col")),
        P(None, ("pt", "row", "col")),
        P(("pt", "row", "col"), None),
    )
    out_specs = (P(("row", "col"), "pt", None), P(("row", "col"), "pt", None))
    return jax.shard_map(body, mesh=mesh, in_specs=in_specs, out_specs=out_specs, check_vma=False)
```

```python
import functools

import jax
import jax.numpy as jnp
from jax import lax
from jax.experimental import pallas as pl
from jax.experimental.pallas import tpu as pltpu
from jax.sharding import PartitionSpec as P

F32 = jnp.float32
BF16 = jnp.bfloat16
MESH = pl.DeviceIdType.MESH

CAMB = 64
DAMPING = 1.0
LANES = 128
TILES = 32
FEATURES = 200
PT_ROW = 144
CAM_ROW = 192
GROUP = 2
WIDTH = 9 * CAMB
NT = (((1,), (1,)), ((), ()))
CHUNKS = 3
ROWS = 72 // CHUNKS
TWO_HOP = 7


def point_factors(pt_ref, out_ref):
    def entry(obs, coordinate, residual):
        return pt_ref[pl.ds((obs * 3 + coordinate) * 32 + residual, 16, stride=2), :]

    sums = {}
    for first in range(3):
        for second in range(first, 3):
            total = None
            for obs in range(8):
                for residual in range(2):
                    term = entry(obs, first, residual) * entry(obs, second, residual)
                    total = term if total is None else total + term
            sums[first, second] = total + DAMPING if first == second else total
    vzz, vzo, vzt = sums[0, 0], sums[0, 1], sums[0, 2]
    voo, vot, vtt = sums[1, 1], sums[1, 2], sums[2, 2]
    adj_zz = voo * vtt - vot * vot
    adj_zo = vzt * vot - vzo * vtt
    adj_zt = vzo * vot - vzt * voo
    adj_oo = vzz * vtt - vzt * vzt
    adj_ot = vzo * vzt - vzz * vot
    adj_tt = vzz * voo - vzo * vzo
    reciprocal = 1.0 / (vzz * adj_zz + vzo * adj_zo + vzt * adj_zt)
    inverse = [
        [entry_ * reciprocal for entry_ in line]
        for line in ((adj_zz, adj_zo, adj_zt), (adj_zo, adj_oo, adj_ot), (adj_zt, adj_ot, adj_tt))
    ]
    for residual in range(2):
        for obs in range(8):
            parts = [entry(obs, coordinate, residual) for coordinate in range(3)]
            for coordinate in range(3):
                if obs < 4:
                    value = (
                        parts[0] * inverse[0][coordinate]
                        + parts[1] * inverse[1][coordinate]
                        + parts[2] * inverse[2][coordinate]
                    )
                else:
                    value = parts[coordinate]
                row = (residual * 24 + obs * 3 + coordinate) * 16
                out_ref[row : row + 16, :] = value


def ranks(tile_ref, member_ref, rank_ref):
    for block in range(16):
        ids = jnp.broadcast_to(tile_ref[block : block + 1, :], (TILES, LANES))
        same = ids == lax.broadcasted_iota(jnp.int32, (TILES, LANES), 0)
        member_ref[block * TILES : (block + 1) * TILES, :] = jnp.where(same, 1.0, 0.0).astype(BF16)
    rows = lax.broadcasted_iota(jnp.int32, (LANES, LANES), 0)
    columns = lax.broadcasted_iota(jnp.int32, (LANES, LANES), 1)
    earlier = jnp.where(rows < columns, 1.0, 0.0).astype(BF16)
    members = member_ref[...]
    before = jnp.dot(members, earlier, preferred_element_type=F32)
    totals = jnp.dot(members, jnp.ones((LANES, LANES), BF16), preferred_element_type=F32)
    base = jnp.zeros((TILES, LANES), F32)
    for block in range(16):
        span = slice(block * TILES, (block + 1) * TILES)
        own = members[span].astype(F32) * (before[span] + base)
        rank_ref[block : block + 1, :] = jnp.sum(own, axis=0, keepdims=True)
        base = base + totals[span]


def gather_features(cam_ref, factor_ref, obs_ref, x_ref):
    for block in range(16):
        lanes = slice(block * LANES, (block + 1) * LANES)
        parts = [cam_ref[pl.ds(block * 2 + residual, 72, stride=32), :] for residual in range(2)]
        parts.append(factor_ref[pl.ds(block, 48, stride=16), :])
        values = jnp.concatenate(parts, axis=0)
        high = values.astype(BF16)
        x_ref[0:192, lanes] = high
        x_ref[208:400, lanes] = (values - high.astype(F32)).astype(BF16)
        names = obs_ref[:, lanes].astype(F32) + 1.0
        x_ref[192:208, lanes] = jnp.concatenate([names, jnp.zeros((8, LANES), F32)], axis=0).astype(BF16)


def place_points(x_ref, tile_ref, rank_ref, place_ref, wanted):
    slots = lax.broadcasted_iota(jnp.int32, (LANES, LANES), 0).astype(F32).astype(BF16)
    one, zero = jnp.ones((LANES, LANES), BF16), jnp.zeros((LANES, LANES), BF16)
    for part in range(2):
        slot_of = jnp.where(tile_ref[...] == wanted[part], rank_ref[...], -1.0)
        for block in range(16):
            row = jnp.broadcast_to(slot_of[block : block + 1, :], (LANES, LANES)).astype(BF16)
            place_ref[part * LANES : (part + 1) * LANES, block * LANES : (block + 1) * LANES] = jnp.where(
                row == slots, one, zero
            )
    placed = lax.dot_general(x_ref[...], place_ref[...], NT, preferred_element_type=F32)
    return placed[0:192] + placed[208:400], placed[192:200]


def fill_factor(block_ref, half, factor_ref, position):
    labels = (lax.broadcasted_iota(jnp.int32, (CAMB, LANES), 0).astype(F32) + 1.0).astype(BF16)
    cameras, masks, cross = [], [], []
    for index in range(4):
        obs = 4 * half + index
        camera = block_ref[CAM_ROW + obs : CAM_ROW + obs + 1, :]
        cameras.append(camera)
        masks.append(labels == jnp.broadcast_to(camera, (CAMB, LANES)).astype(BF16))
        camera_rows = [block_ref[res * 72 + obs * 9 : res * 72 + obs * 9 + 9, :] for res in range(2)]
        line = []
        for coordinate in range(3):
            rows = [PT_ROW + res * 24 + obs * 3 + coordinate for res in range(2)]
            line.append(
                camera_rows[0] * block_ref[rows[0] : rows[0] + 1, :]
                + camera_rows[1] * block_ref[rows[1] : rows[1] + 1, :]
            )
        cross.append(line)
    for index in range(4):
        for later in range(index + 1, 4):
            same = cameras[index] == cameras[later]
            for coordinate in range(3):
                cross[index][coordinate] = cross[index][coordinate] + jnp.where(same, cross[later][coordinate], 0.0)
    for coordinate in range(3):
        first = (coordinate * GROUP + position) * LANES
        for parameter in range(9):
            value = jnp.zeros((CAMB, LANES), BF16)
            for index in (3, 2, 1, 0):
                row = cross[index][coordinate][parameter : parameter + 1, :]
                value = jnp.where(masks[index], jnp.broadcast_to(row, (CAMB, LANES)).astype(BF16), value)
            factor_ref[parameter * CAMB : (parameter + 1) * CAMB, first : first + LANES] = value


def split_three(value):
    high = value.astype(BF16)
    rest = value - high.astype(F32)
    middle = rest.astype(BF16)
    return high, middle, (rest - middle.astype(F32)).astype(BF16)


def permute_columns(value, perm_ref):
    stacked = jnp.concatenate(split_three(value), axis=0)
    ordered = lax.dot_general(stacked, perm_ref[...], NT, preferred_element_type=F32)
    rows = value.shape[0]
    return ordered[0:rows] + ordered[rows : 2 * rows] + ordered[2 * rows :]


def kernel(
    cam_hbm, pt_hbm, obs_hbm, tile_hbm, upper_ref, lower_ref,
    cam_ref, pt_ref, obs_ref, tile_ref,
    x_ref, factor_ref, member_ref, rank_ref, place_ref, sent_ref, held_ref, relay_ref, left_ref, right_ref,
    total_ref, chain_a, chain_b, piece_ref, folded_ref, row_mid, row_got, flip_ref, flip_mid, flip_got, lanes_ref,
    load_sem, sent_sem, held_sem, relay_sem, again_sem, chain_sent, chain_held, mid_sent, mid_held, end_sent, end_held, last_sem,
):
    pt, row, col = lax.axis_index("pt"), lax.axis_index("row"), lax.axis_index("col")
    y, core = pt // 2, lax.rem(pt, 2)

    loads = [
        pltpu.make_async_copy(source, target, load_sem.at[index])
        for index, (source, target) in enumerate(
            ((tile_hbm, tile_ref), (pt_hbm, pt_ref), (obs_hbm, obs_ref), (cam_hbm, cam_ref))
        )
    ]
    for load in loads:
        load.start()

    def device(shift_y, shift_x, part):
        return (lax.rem(y + shift_y, 4) * 2 + (core if part == 0 else 1 - core), row, lax.rem(col + shift_x, 4))

    barrier = pltpu.get_barrier_semaphore()

    def greet(there):
        pl.semaphore_signal(barrier, inc=1, device_id=there, device_id_type=MESH)

    for part in range(2):
        for shift in range(1, 4):
            greet(device(0, shift, part))
            greet(device(shift, 0, part))
    greet(device(0, 0, 1))
    greet((pt, lax.rem(row + 1, 8), col))
    greet((pt, lax.rem(row + 7, 8), col))

    loads[0].wait()
    ranks(tile_ref, member_ref, rank_ref)
    loads[1].wait()
    point_factors(pt_ref, factor_ref)
    loads[2].wait()
    loads[3].wait()
    gather_features(cam_ref, factor_ref, obs_ref, x_ref)

    pl.semaphore_wait(barrier, 15)

    def single(index):
        far, along = index // 2 + 1, lax.rem(index, 2)
        return along * far, (1 - along) * far

    def double(index):
        return lax.rem(index + index // 3, 3) + 1, lax.rem(index, 3) + 1

    def direct(block, there):
        return pltpu.make_async_remote_copy(
            src_ref=sent_ref.at[block],
            dst_ref=held_ref.at[block],
            send_sem=sent_sem.at[block],
            recv_sem=held_sem.at[block],
            device_id=there,
            device_id_type=MESH,
        )

    def first_hop(block, there):
        return pltpu.make_async_remote_copy(
            src_ref=sent_ref.at[block],
            dst_ref=relay_ref.at[block - 2 * TWO_HOP],
            send_sem=sent_sem.at[block],
            recv_sem=relay_sem.at[block - 2 * TWO_HOP],
            device_id=there,
            device_id_type=MESH,
        )

    def second_hop(block, there):
        return pltpu.make_async_remote_copy(
            src_ref=relay_ref.at[block - 2 * TWO_HOP],
            dst_ref=held_ref.at[block],
            send_sem=again_sem.at[block - 2 * TWO_HOP],
            recv_sem=held_sem.at[block],
            device_id=there,
            device_id_type=MESH,
        )

    def place_pair(shift_y, shift_x):
        owners = [device(shift_y, shift_x, part) for part in range(2)]
        wanted = [owner[0] * 4 + owner[2] for owner in owners]
        placed, names = place_points(x_ref, tile_ref, rank_ref, place_ref, wanted)
        return owners, placed, names

    def store(target, block, placed, names, part):
        lanes = slice(part * LANES, (part + 1) * LANES)
        target[block, 0:192, :] = placed[:, lanes]
        target[block, 192:200, :] = names[:, lanes]

    def send_single(index, _):
        owners, placed, names = place_pair(*single(index))
        for part in range(2):
            block = 2 * (index + 1) + part
            store(sent_ref, block, placed, names, part)
            direct(block, owners[part]).start()
        return 0

    def send_double(index, _):
        shift_y, shift_x = double(index)
        _, placed, names = place_pair(shift_y, shift_x)
        block = 2 * (index + TWO_HOP)
        store(sent_ref, block, placed, names, 0)
        first_hop(block, device(0, shift_x, 0)).start()
        store(sent_ref, block + 1, placed, names, 1)
        first_hop(block + 1, device(shift_y, 0, 0)).start()
        return 0

    def forward(index, _):
        shift_y, shift_x = double(index)
        block = 2 * (index + TWO_HOP)
        first_hop(block, (pt, row, col)).wait_recv()
        second_hop(block, device(shift_y, 0, 0)).start()
        first_hop(block + 1, (pt, row, col)).wait_recv()
        second_hop(block + 1, device(0, shift_x, 1)).start()
        return 0

    lax.fori_loop(0, 9, send_double, 0)
    lax.fori_loop(0, 6, send_single, 0)
    lax.fori_loop(0, 3, forward, 0)
    owners, placed, names = place_pair(0, 0)
    store(held_ref, 0, placed, names, 0)
    store(sent_ref, 1, placed, names, 1)
    direct(1, owners[1]).start()

    folded_ref[...] = jnp.zeros_like(folded_ref)
    total_ref[...] = jnp.zeros_like(total_ref)

    def add_group(group, _):
        start = jnp.minimum(2 * group + 3, 9)
        stop = jnp.minimum(2 * group + 5, 9)
        lax.fori_loop(start, stop, forward, 0)
        for position in range(GROUP):
            index = group * GROUP + position

            @pl.when(index > 0)
            def _():
                direct(index, (pt, row, col)).wait_recv()

        for position in range(GROUP):
            block = held_ref.at[group * GROUP + position]
            fill_factor(block, 0, left_ref, position)
            fill_factor(block, 1, right_ref, position)
        product = lax.dot_general(left_ref[...], right_ref[...], NT, preferred_element_type=F32)
        total_ref[:, 0:64, :] -= product[0:512].reshape(8, 64, WIDTH)
        total_ref[:, 64:72, :] -= product[512:576].reshape(8, 8, WIDTH)
        return 0

    lax.fori_loop(0, TILES // GROUP, add_group, 0)

    ways = (jnp.where(core == 0, 1, 7), jnp.where(core == 0, 7, 1))
    chains = (chain_a, chain_b)
    hops = (4, 3)

    def piece_at(side, distance):
        return lax.rem(row + distance * ways[side], 8)

    def hop(side, step, chunk):
        span = slice(chunk * ROWS, (chunk + 1) * ROWS)
        source_ref = total_ref.at[piece_at(side, hops[side]), span] if step == 0 else chains[side].at[step - 1, span]
        return pltpu.make_async_remote_copy(
            src_ref=source_ref,
            dst_ref=chains[side].at[step, span],
            send_sem=chain_sent.at[side, step, chunk],
            recv_sem=chain_held.at[side, step, chunk],
            device_id=(pt, piece_at(side, 1), col),
            device_id_type=MESH,
        )

    mirror = lax.rem(row + 4, 8)
    middles = (row_mid, flip_mid)
    ends = (row_got, flip_got)

    def block_of(kind, other):
        if kind == 1:
            return flip_ref.at[other]
        return piece_ref.at[pl.ds(pl.multiple_of(other * 8, 8), 8), :]

    def to_middle(kind, other, slot):
        return pltpu.make_async_remote_copy(
            src_ref=block_of(kind, other),
            dst_ref=middles[kind].at[slot],
            send_sem=mid_sent.at[kind, other],
            recv_sem=mid_held.at[kind, slot],
            device_id=(other, row, col),
            device_id_type=MESH,
        )

    def to_end(kind, other, slot):
        return pltpu.make_async_remote_copy(
            src_ref=middles[kind].at[other],
            dst_ref=ends[kind].at[slot],
            send_sem=end_sent.at[kind, other],
            recv_sem=end_held.at[kind, slot],
            device_id=(pt, other if kind == 0 else lax.rem(other + 4, 8), col),
            device_id_type=MESH,
        )

    last_row = pltpu.make_async_remote_copy(
        src_ref=piece_ref.at[64:72, :],
        dst_ref=row_got.at[8],
        send_sem=last_sem.at[0],
        recv_sem=last_sem.at[1],
        device_id=(row, pt, col),
        device_id_type=MESH,
    )

    def start_middle(kind, first, last):
        def start(other, _):
            @pl.when(other != pt)
            def _():
                to_middle(kind, other, pt).start()

            @pl.when(other == pt)
            def _():
                middles[kind][other] = block_of(kind, other)[...]

            return 0

        lax.fori_loop(first, last, start, 0)

    def start_end(kind):
        own = row if kind == 0 else mirror

        def start(index, _):
            other = lax.rem(pt + index, 8)

            @pl.when(other != pt)
            def _():
                to_middle(kind, other, other).wait_recv()

            @pl.when(other != own)
            def _():
                to_end(kind, other, row).start()

            @pl.when(other == own)
            def _():
                ends[kind][row] = middles[kind][other]

            return 0

        lax.fori_loop(0, 8, start, 0)

    for chunk in range(CHUNKS):
        for side in range(2):
            hop(side, 0, chunk).start()
    for step in range(3):
        for chunk in range(CHUNKS):
            span = slice(chunk * ROWS, (chunk + 1) * ROWS)
            for side in range(2):
                if step < hops[side] - 1:
                    hop(side, step, chunk).wait_recv()
                    mine = total_ref[piece_at(side, hops[side] - 1 - step), span, :]
                    chains[side][step, span, :] = chains[side][step, span, :] + mine
                    hop(side, step + 1, chunk).start()
    for chunk in range(CHUNKS):
        span = slice(chunk * ROWS, (chunk + 1) * ROWS)
        hop(1, 2, chunk).wait_recv()
        hop(0, 3, chunk).wait_recv()
        piece_ref[span, :] = chain_a[3, span, :] + chain_b[2, span, :] + total_ref[row, span, :]
        start_middle(0, chunk * ROWS // 8, min((chunk + 1) * ROWS // 8, 8))

    @pl.when(pt != row)
    def _():
        last_row.start()

    @pl.when(pt == row)
    def _():
        row_got[8] = piece_ref[64:72, :]

    folded_ref[0:64, 0:256] = piece_ref[0:64, 0:256]
    folded_ref[64:128, 0:256] = piece_ref[0:64, 256:512]
    folded_ref[0:64, 256:320] = piece_ref[0:64, 512:576]
    for parameter in range(8):
        folded_ref[64 + parameter * 8 : 72 + parameter * 8, 256:320] = piece_ref[
            64:72, parameter * 64 : (parameter + 1) * 64
        ]
    folded_ref[0:8, 320:384] = piece_ref[64:72, 512:576]
    flipped = folded_ref[...].T
    for other in range(8):
        for tile in range(6):
            first = tile * CAMB + other * 8
            flip_ref[other, tile] = flipped[first : first + 8, :]
    start_middle(1, 0, 8)
    start_end(0)
    start_end(1)

    for other in range(8):
        @pl.when(row != other)
        def _():
            to_end(0, other, other).wait_recv()

    @pl.when(pt != row)
    def _():
        last_row.wait_recv()

    upper_ref[...] = row_got[...].reshape(72, WIDTH)

    for other in range(8):
        @pl.when(row != other)
        def _():
            to_end(1, other, other).wait_recv()

        for parameter in range(9):
            rows = slice(parameter * 8, (parameter + 1) * 8)
            tile, lane = (4, 0) if parameter == 8 else (parameter % 4, parameter // 4 * 64)
            lanes_ref[rows, other * 64 : (other + 1) * 64] = flip_got[other, tile, :, lane : lane + 64]
            tile, lane = (5, 0) if parameter == 8 else (4, 64 + parameter * 8)
            lanes_ref[rows, 512 + other * 8 : 520 + other * 8] = flip_got[other, tile, :, lane : lane + 8]
    lower_ref[...] = lanes_ref[...]

    def drain(block, _):
        direct(block, (pt, row, col)).wait_send()
        return 0

    def drain_again(block, _):
        second_hop(block, (pt, row, col)).wait_send()
        return 0

    lax.fori_loop(1, TILES, drain, 0)
    lax.fori_loop(2 * TWO_HOP, TILES, drain_again, 0)
    for side in range(2):
        for step in range(hops[side]):
            for chunk in range(CHUNKS):
                hop(side, step, chunk).wait_send()

    @pl.when(pt != row)
    def _():
        last_row.wait_send()

    def drain_blocks(other, _):
        for kind in range(2):

            @pl.when(other != pt)
            def _(kind=kind):
                to_middle(kind, other, pt).wait_send()

            @pl.when(other != (row if kind == 0 else mirror))
            def _(kind=kind):
                to_end(kind, other, row).wait_send()

        return 0

    lax.fori_loop(0, 8, drain_blocks, 0)


def order(upper_in, lower_in, upper_ref, lower_ref, perm_ref):
    source = lax.broadcasted_iota(jnp.int32, (WIDTH, WIDTH), 1)
    goal = lax.broadcasted_iota(jnp.int32, (WIDTH, WIDTH), 0)
    perm_ref[...] = jnp.where((source & 63) * 9 + (source >> 6) == goal, 1.0, 0.0).astype(BF16)

    def write_rows(target_ref, value):
        for parameter in range(9):
            for camera in range(8):
                goal_row, source_row = camera * 9 + parameter, parameter * 8 + camera
                target_ref[goal_row : goal_row + 1, :] = value[source_row : source_row + 1]

    write_rows(upper_ref, permute_columns(upper_in[...], perm_ref))
    write_rows(lower_ref, permute_columns(lower_in[...], perm_ref))


def body(jac_cam, jac_pt, obs_cam, point_covisible_tile):
    def rows_of(array):
        observed, _, width, held = array.shape
        array = array.transpose(0, 2, 1, 3).reshape(observed * width, 2, held // LANES, LANES)
        return array.transpose(0, 2, 1, 3).reshape(observed * width * 2 * held // LANES, LANES)

    vmem = pl.BlockSpec(memory_space=pltpu.VMEM)
    upper, lower = pl.pallas_call(
        kernel,
        out_shape=[jax.ShapeDtypeStruct((72, WIDTH), F32)] * 2,
        in_specs=[pl.BlockSpec(memory_space=pl.ANY)] * 4,
        out_specs=[vmem] * 2,
        scratch_shapes=[
            pltpu.VMEM((2304, LANES), F32),
            pltpu.VMEM((768, LANES), F32),
            pltpu.VMEM((8, 2048), jnp.int32),
            pltpu.VMEM((16, LANES), jnp.int32),
            pltpu.VMEM((400, 2048), BF16),
            pltpu.VMEM((768, LANES), F32),
            pltpu.VMEM((512, LANES), BF16),
            pltpu.VMEM((16, LANES), F32),
            pltpu.VMEM((256, 2048), BF16),
            pltpu.VMEM((TILES, FEATURES, LANES), F32),
            pltpu.VMEM((TILES, FEATURES, LANES), F32),
            pltpu.VMEM((18, FEATURES, LANES), F32),
            pltpu.VMEM((WIDTH, 3 * LANES * GROUP), BF16),
            pltpu.VMEM((WIDTH, 3 * LANES * GROUP), BF16),
            pltpu.VMEM((8, 72, WIDTH), F32),
            pltpu.VMEM((4, 72, WIDTH), F32),
            pltpu.VMEM((3, 72, WIDTH), F32),
            pltpu.VMEM((72, WIDTH), F32),
            pltpu.VMEM((LANES, 384), F32),
            pltpu.VMEM((8, 8, WIDTH), F32),
            pltpu.VMEM((9, 8, WIDTH), F32),
            pltpu.VMEM((8, 6, 8, LANES), F32),
            pltpu.VMEM((8, 6, 8, LANES), F32),
            pltpu.VMEM((8, 6, 8, LANES), F32),
            pltpu.VMEM((72, WIDTH), F32),
            pltpu.SemaphoreType.DMA((4,)),
            pltpu.SemaphoreType.DMA((TILES,)),
            pltpu.SemaphoreType.DMA((TILES,)),
            pltpu.SemaphoreType.DMA((18,)),
            pltpu.SemaphoreType.DMA((18,)),
            pltpu.SemaphoreType.DMA((2, 4, CHUNKS)),
            pltpu.SemaphoreType.DMA((2, 4, CHUNKS)),
            pltpu.SemaphoreType.DMA((2, 8)),
            pltpu.SemaphoreType.DMA((2, 8)),
            pltpu.SemaphoreType.DMA((2, 8)),
            pltpu.SemaphoreType.DMA((2, 8)),
            pltpu.SemaphoreType.DMA((2,)),
        ],
        compiler_params=pltpu.CompilerParams(
            collective_id=0, has_side_effects=True, vmem_limit_bytes=64 * 2**20 - 2**19
        ),
    )(rows_of(jac_cam), rows_of(jac_pt), obs_cam, point_covisible_tile.reshape(16, LANES))
    upper, lower = pl.pallas_call(
        order,
        out_shape=[jax.ShapeDtypeStruct((72, WIDTH), F32)] * 2,
        in_specs=[vmem] * 2,
        out_specs=[vmem] * 2,
        scratch_shapes=[pltpu.VMEM((WIDTH, WIDTH), BF16)],
        compiler_params=pltpu.CompilerParams(vmem_limit_bytes=64 * 2**20 - 2**19),
    )(upper, lower)
    return (upper[None], lower[None])


def solution(mesh):
    in_specs = (
        P(None, None, None, ("pt", "row", "col")),
        P(None, None, None, ("pt", "row", "col")),
        P(None, ("pt", "row", "col")),
        P(("pt", "row", "col"), None),
    )
    out_specs = (P(("row", "col"), "pt", None), P(("row", "col"), "pt", None))
    return jax.shard_map(body, mesh=mesh, in_specs=in_specs, out_specs=out_specs, check_vma=False)
```

```python
import functools

import jax
import jax.numpy as jnp
from jax import lax
from jax.experimental import pallas as pl
from jax.experimental.pallas import tpu as pltpu
from jax.sharding import PartitionSpec as P

F32 = jnp.float32
BF16 = jnp.bfloat16
MESH = pl.DeviceIdType.MESH

CAMB = 64
DAMPING = 1.0
LANES = 128
TILES = 32
FEATURES = 200
PT_ROW = 144
CAM_ROW = 192
GROUP = 2
WIDTH = 9 * CAMB
NT = (((1,), (1,)), ((), ()))
CHUNKS = 3
ROWS = 72 // CHUNKS
TWO_HOP = 7


def point_factors(pt_ref, out_ref):
    def entry(obs, coordinate, residual):
        return pt_ref[pl.ds((obs * 3 + coordinate) * 32 + residual, 16, stride=2), :]

    sums = {}
    for first in range(3):
        for second in range(first, 3):
            total = None
            for obs in range(8):
                for residual in range(2):
                    term = entry(obs, first, residual) * entry(obs, second, residual)
                    total = term if total is None else total + term
            sums[first, second] = total + DAMPING if first == second else total
    vzz, vzo, vzt = sums[0, 0], sums[0, 1], sums[0, 2]
    voo, vot, vtt = sums[1, 1], sums[1, 2], sums[2, 2]
    adj_zz = voo * vtt - vot * vot
    adj_zo = vzt * vot - vzo * vtt
    adj_zt = vzo * vot - vzt * voo
    adj_oo = vzz * vtt - vzt * vzt
    adj_ot = vzo * vzt - vzz * vot
    adj_tt = vzz * voo - vzo * vzo
    reciprocal = 1.0 / (vzz * adj_zz + vzo * adj_zo + vzt * adj_zt)
    inverse = [
        [entry_ * reciprocal for entry_ in line]
        for line in ((adj_zz, adj_zo, adj_zt), (adj_zo, adj_oo, adj_ot), (adj_zt, adj_ot, adj_tt))
    ]
    for residual in range(2):
        for obs in range(8):
            parts = [entry(obs, coordinate, residual) for coordinate in range(3)]
            for coordinate in range(3):
                if obs < 4:
                    value = (
                        parts[0] * inverse[0][coordinate]
                        + parts[1] * inverse[1][coordinate]
                        + parts[2] * inverse[2][coordinate]
                    )
                else:
                    value = parts[coordinate]
                row = (residual * 24 + obs * 3 + coordinate) * 16
                out_ref[row : row + 16, :] = value


def ranks(tile_ref, member_ref, rank_ref):
    for block in range(16):
        ids = jnp.broadcast_to(tile_ref[block : block + 1, :], (TILES, LANES))
        same = ids == lax.broadcasted_iota(jnp.int32, (TILES, LANES), 0)
        member_ref[block * TILES : (block + 1) * TILES, :] = jnp.where(same, 1.0, 0.0).astype(BF16)
    rows = lax.broadcasted_iota(jnp.int32, (LANES, LANES), 0)
    columns = lax.broadcasted_iota(jnp.int32, (LANES, LANES), 1)
    earlier = jnp.where(rows < columns, 1.0, 0.0).astype(BF16)
    members = member_ref[...]
    before = jnp.dot(members, earlier, preferred_element_type=F32)
    totals = jnp.dot(members, jnp.ones((LANES, LANES), BF16), preferred_element_type=F32)
    base = jnp.zeros((TILES, LANES), F32)
    for block in range(16):
        span = slice(block * TILES, (block + 1) * TILES)
        own = members[span].astype(F32) * (before[span] + base)
        rank_ref[block : block + 1, :] = jnp.sum(own, axis=0, keepdims=True)
        base = base + totals[span]


def gather_features(cam_ref, factor_ref, obs_ref, x_ref):
    for block in range(16):
        lanes = slice(block * LANES, (block + 1) * LANES)
        parts = [cam_ref[pl.ds(block * 2 + residual, 72, stride=32), :] for residual in range(2)]
        parts.append(factor_ref[pl.ds(block, 48, stride=16), :])
        values = jnp.concatenate(parts, axis=0)
        high = values.astype(BF16)
        x_ref[0:192, lanes] = high
        x_ref[208:400, lanes] = (values - high.astype(F32)).astype(BF16)
        names = obs_ref[:, lanes].astype(F32) + 1.0
        x_ref[192:208, lanes] = jnp.concatenate([names, jnp.zeros((8, LANES), F32)], axis=0).astype(BF16)


def place_points(x_ref, tile_ref, rank_ref, place_ref, wanted):
    slots = lax.broadcasted_iota(jnp.int32, (LANES, LANES), 0).astype(F32).astype(BF16)
    one, zero = jnp.ones((LANES, LANES), BF16), jnp.zeros((LANES, LANES), BF16)
    for part in range(2):
        slot_of = jnp.where(tile_ref[...] == wanted[part], rank_ref[...], -1.0)
        for block in range(16):
            row = jnp.broadcast_to(slot_of[block : block + 1, :], (LANES, LANES)).astype(BF16)
            place_ref[part * LANES : (part + 1) * LANES, block * LANES : (block + 1) * LANES] = jnp.where(
                row == slots, one, zero
            )
    placed = lax.dot_general(x_ref[...], place_ref[...], NT, preferred_element_type=F32)
    return placed[0:192] + placed[208:400], placed[192:200]


def fill_factor(block_ref, half, factor_ref, position):
    labels = (lax.broadcasted_iota(jnp.int32, (CAMB, LANES), 0).astype(F32) + 1.0).astype(BF16)
    cameras, masks, cross = [], [], []
    for index in range(4):
        obs = 4 * half + index
        camera = block_ref[CAM_ROW + obs : CAM_ROW + obs + 1, :]
        cameras.append(camera)
        masks.append(labels == jnp.broadcast_to(camera, (CAMB, LANES)).astype(BF16))
        camera_rows = [block_ref[res * 72 + obs * 9 : res * 72 + obs * 9 + 9, :] for res in range(2)]
        line = []
        for coordinate in range(3):
            rows = [PT_ROW + res * 24 + obs * 3 + coordinate for res in range(2)]
            line.append(
                camera_rows[0] * block_ref[rows[0] : rows[0] + 1, :]
                + camera_rows[1] * block_ref[rows[1] : rows[1] + 1, :]
            )
        cross.append(line)
    for index in range(4):
        for later in range(index + 1, 4):
            same = cameras[index] == cameras[later]
            for coordinate in range(3):
                cross[index][coordinate] = cross[index][coordinate] + jnp.where(same, cross[later][coordinate], 0.0)
    for coordinate in range(3):
        first = (coordinate * GROUP + position) * LANES
        for parameter in range(9):
            value = jnp.zeros((CAMB, LANES), BF16)
            for index in (3, 2, 1, 0):
                row = cross[index][coordinate][parameter : parameter + 1, :]
                value = jnp.where(masks[index], jnp.broadcast_to(row, (CAMB, LANES)).astype(BF16), value)
            factor_ref[parameter * CAMB : (parameter + 1) * CAMB, first : first + LANES] = value


def split_three(value):
    high = value.astype(BF16)
    rest = value - high.astype(F32)
    middle = rest.astype(BF16)
    return high, middle, (rest - middle.astype(F32)).astype(BF16)


def permute_columns(value, perm_ref):
    stacked = jnp.concatenate(split_three(value), axis=0)
    ordered = lax.dot_general(stacked, perm_ref[...], NT, preferred_element_type=F32)
    rows = value.shape[0]
    return ordered[0:rows] + ordered[rows : 2 * rows] + ordered[2 * rows :]


def kernel(
    cam_hbm, pt_hbm, obs_hbm, tile_hbm, upper_ref, lower_ref,
    cam_ref, pt_ref, obs_ref, tile_ref,
    x_ref, factor_ref, member_ref, rank_ref, place_ref, sent_ref, held_ref, relay_ref, left_ref, right_ref,
    total_ref, chain_a, chain_b, piece_ref, folded_ref, row_mid, row_got, flip_ref, flip_mid, flip_got, lanes_ref,
    load_sem, sent_sem, held_sem, relay_sem, again_sem, chain_sent, chain_held, mid_sent, mid_held, end_sent, end_held, last_sem,
):
    pt, row, col = lax.axis_index("pt"), lax.axis_index("row"), lax.axis_index("col")
    y, core = pt // 2, lax.rem(pt, 2)

    loads = [
        pltpu.make_async_copy(source, target, load_sem.at[index])
        for index, (source, target) in enumerate(
            ((tile_hbm, tile_ref), (pt_hbm, pt_ref), (obs_hbm, obs_ref), (cam_hbm, cam_ref))
        )
    ]
    for load in loads:
        load.start()

    def device(shift_y, shift_x, part):
        return (lax.rem(y + shift_y, 4) * 2 + (core if part == 0 else 1 - core), row, lax.rem(col + shift_x, 4))

    barrier = pltpu.get_barrier_semaphore()

    def greet(there):
        pl.semaphore_signal(barrier, inc=1, device_id=there, device_id_type=MESH)

    for part in range(2):
        for shift in range(1, 4):
            greet(device(0, shift, part))
            greet(device(shift, 0, part))
    greet(device(0, 0, 1))
    greet((pt, lax.rem(row + 1, 8), col))
    greet((pt, lax.rem(row + 7, 8), col))

    loads[0].wait()
    ranks(tile_ref, member_ref, rank_ref)
    loads[1].wait()
    point_factors(pt_ref, factor_ref)
    loads[2].wait()
    loads[3].wait()
    gather_features(cam_ref, factor_ref, obs_ref, x_ref)

    pl.semaphore_wait(barrier, 15)

    def single(index):
        far, along = index // 2 + 1, lax.rem(index, 2)
        return along * far, (1 - along) * far

    def double(index):
        return lax.rem(index + index // 3, 3) + 1, lax.rem(index, 3) + 1

    def direct(block, there):
        return pltpu.make_async_remote_copy(
            src_ref=sent_ref.at[block],
            dst_ref=held_ref.at[block],
            send_sem=sent_sem.at[block],
            recv_sem=held_sem.at[block],
            device_id=there,
            device_id_type=MESH,
        )

    def first_hop(block, there):
        return pltpu.make_async_remote_copy(
            src_ref=sent_ref.at[block],
            dst_ref=relay_ref.at[block - 2 * TWO_HOP],
            send_sem=sent_sem.at[block],
            recv_sem=relay_sem.at[block - 2 * TWO_HOP],
            device_id=there,
            device_id_type=MESH,
        )

    def second_hop(block, there):
        return pltpu.make_async_remote_copy(
            src_ref=relay_ref.at[block - 2 * TWO_HOP],
            dst_ref=held_ref.at[block],
            send_sem=again_sem.at[block - 2 * TWO_HOP],
            recv_sem=held_sem.at[block],
            device_id=there,
            device_id_type=MESH,
        )

    def place_pair(shift_y, shift_x):
        owners = [device(shift_y, shift_x, part) for part in range(2)]
        wanted = [owner[0] * 4 + owner[2] for owner in owners]
        placed, names = place_points(x_ref, tile_ref, rank_ref, place_ref, wanted)
        return owners, placed, names

    def store(target, block, placed, names, part):
        lanes = slice(part * LANES, (part + 1) * LANES)
        target[block, 0:192, :] = placed[:, lanes]
        target[block, 192:200, :] = names[:, lanes]

    def send_single(index, _):
        owners, placed, names = place_pair(*single(index))
        for part in range(2):
            block = 2 * (index + 1) + part
            store(sent_ref, block, placed, names, part)
            direct(block, owners[part]).start()
        return 0

    def send_double(index, _):
        shift_y, shift_x = double(index)
        _, placed, names = place_pair(shift_y, shift_x)
        block = 2 * (index + TWO_HOP)
        store(sent_ref, block, placed, names, 0)
        first_hop(block, device(0, shift_x, 0)).start()
        store(sent_ref, block + 1, placed, names, 1)
        first_hop(block + 1, device(shift_y, 0, 0)).start()
        return 0

    def forward(index, _):
        shift_y, shift_x = double(index)
        block = 2 * (index + TWO_HOP)
        first_hop(block, (pt, row, col)).wait_recv()
        second_hop(block, device(shift_y, 0, 0)).start()
        first_hop(block + 1, (pt, row, col)).wait_recv()
        second_hop(block + 1, device(0, shift_x, 1)).start()
        return 0

    lax.fori_loop(0, 9, send_double, 0)
    lax.fori_loop(0, 6, send_single, 0)
    lax.fori_loop(0, 3, forward, 0)
    owners, placed, names = place_pair(0, 0)
    store(held_ref, 0, placed, names, 0)
    store(sent_ref, 1, placed, names, 1)
    direct(1, owners[1]).start()

    folded_ref[...] = jnp.zeros_like(folded_ref)
    total_ref[...] = jnp.zeros_like(total_ref)

    def add_group(group, _):
        start = jnp.minimum(2 * group + 3, 9)
        stop = jnp.minimum(2 * group + 5, 9)
        lax.fori_loop(start, stop, forward, 0)
        for position in range(GROUP):
            index = group * GROUP + position

            @pl.when(index > 0)
            def _():
                direct(index, (pt, row, col)).wait_recv()

        for position in range(GROUP):
            block = held_ref.at[group * GROUP + position]
            fill_factor(block, 0, left_ref, position)
            fill_factor(block, 1, right_ref, position)
        product = lax.dot_general(left_ref[...], right_ref[...], NT, preferred_element_type=F32)
        total_ref[:, 0:64, :] -= product[0:512].reshape(8, 64, WIDTH)
        total_ref[:, 64:72, :] -= product[512:576].reshape(8, 8, WIDTH)
        return 0

    lax.fori_loop(0, TILES // GROUP, add_group, 0)

    ways = (jnp.where(core == 0, 1, 7), jnp.where(core == 0, 7, 1))
    chains = (chain_a, chain_b)
    hops = (4, 3)

    def piece_at(side, distance):
        return lax.rem(row + distance * ways[side], 8)

    def hop(side, step, chunk):
        span = slice(chunk * ROWS, (chunk + 1) * ROWS)
        source_ref = total_ref.at[piece_at(side, hops[side]), span] if step == 0 else chains[side].at[step - 1, span]
        return pltpu.make_async_remote_copy(
            src_ref=source_ref,
            dst_ref=chains[side].at[step, span],
            send_sem=chain_sent.at[side, step, chunk],
            recv_sem=chain_held.at[side, step, chunk],
            device_id=(pt, piece_at(side, 1), col),
            device_id_type=MESH,
        )

    mirror = lax.rem(row + 4, 8)
    middles = (row_mid, flip_mid)
    ends = (row_got, flip_got)

    def block_of(kind, other):
        if kind == 1:
            return flip_ref.at[other]
        return piece_ref.at[pl.ds(pl.multiple_of(other * 8, 8), 8), :]

    def to_middle(kind, other, slot):
        return pltpu.make_async_remote_copy(
            src_ref=block_of(kind, other),
            dst_ref=middles[kind].at[slot],
            send_sem=mid_sent.at[kind, other],
            recv_sem=mid_held.at[kind, slot],
            device_id=(other, row, col),
            device_id_type=MESH,
        )

    def to_end(kind, other, slot):
        return pltpu.make_async_remote_copy(
            src_ref=middles[kind].at[other],
            dst_ref=ends[kind].at[slot],
            send_sem=end_sent.at[kind, other],
            recv_sem=end_held.at[kind, slot],
            device_id=(pt, other if kind == 0 else lax.rem(other + 4, 8), col),
            device_id_type=MESH,
        )

    last_row = pltpu.make_async_remote_copy(
        src_ref=piece_ref.at[64:72, :],
        dst_ref=row_got.at[8],
        send_sem=last_sem.at[0],
        recv_sem=last_sem.at[1],
        device_id=(row, pt, col),
        device_id_type=MESH,
    )

    def start_middle(kind, first, last):
        def start(other, _):
            @pl.when(other != pt)
            def _():
                to_middle(kind, other, pt).start()

            @pl.when(other == pt)
            def _():
                middles[kind][other] = block_of(kind, other)[...]

            return 0

        lax.fori_loop(first, last, start, 0)

    def start_end(kind):
        own = row if kind == 0 else mirror

        def start(index, _):
            other = lax.rem(pt + index, 8)

            @pl.when(other != pt)
            def _():
                to_middle(kind, other, other).wait_recv()

            @pl.when(other != own)
            def _():
                to_end(kind, other, row).start()

            @pl.when(other == own)
            def _():
                ends[kind][row] = middles[kind][other]

            return 0

        lax.fori_loop(0, 8, start, 0)

    for chunk in range(CHUNKS):
        for side in range(2):
            hop(side, 0, chunk).start()

    def drain(block, _):
        direct(block, (pt, row, col)).wait_send()
        return 0

    def drain_again(block, _):
        second_hop(block, (pt, row, col)).wait_send()
        return 0

    lax.fori_loop(1, TILES, drain, 0)
    lax.fori_loop(2 * TWO_HOP, TILES, drain_again, 0)

    for step in range(3):
        for chunk in range(CHUNKS):
            span = slice(chunk * ROWS, (chunk + 1) * ROWS)
            for side in range(2):
                if step < hops[side] - 1:
                    hop(side, step, chunk).wait_recv()
                    mine = total_ref[piece_at(side, hops[side] - 1 - step), span, :]
                    chains[side][step, span, :] = chains[side][step, span, :] + mine
                    hop(side, step + 1, chunk).start()
    for chunk in range(CHUNKS):
        span = slice(chunk * ROWS, (chunk + 1) * ROWS)
        hop(1, 2, chunk).wait_recv()
        hop(0, 3, chunk).wait_recv()
        piece_ref[span, :] = chain_a[3, span, :] + chain_b[2, span, :] + total_ref[row, span, :]
        start_middle(0, chunk * ROWS // 8, min((chunk + 1) * ROWS // 8, 8))

    @pl.when(pt != row)
    def _():
        last_row.start()

    @pl.when(pt == row)
    def _():
        row_got[8] = piece_ref[64:72, :]

    folded_ref[0:64, 0:256] = piece_ref[0:64, 0:256]
    folded_ref[64:128, 0:256] = piece_ref[0:64, 256:512]
    folded_ref[0:64, 256:320] = piece_ref[0:64, 512:576]
    for parameter in range(8):
        folded_ref[64 + parameter * 8 : 72 + parameter * 8, 256:320] = piece_ref[
            64:72, parameter * 64 : (parameter + 1) * 64
        ]
    folded_ref[0:8, 320:384] = piece_ref[64:72, 512:576]
    flipped = folded_ref[...].T
    for other in range(8):
        for tile in range(6):
            first = tile * CAMB + other * 8
            flip_ref[other, tile] = flipped[first : first + 8, :]
    start_middle(1, 0, 8)
    start_end(0)
    start_end(1)
    for side in range(2):
        for step in range(hops[side]):
            for chunk in range(CHUNKS):
                hop(side, step, chunk).wait_send()

    for other in range(8):
        @pl.when(row != other)
        def _():
            to_end(0, other, other).wait_recv()

    @pl.when(pt != row)
    def _():
        last_row.wait_recv()

    upper_ref[...] = row_got[...].reshape(72, WIDTH)

    for other in range(8):
        @pl.when(row != other)
        def _():
            to_end(1, other, other).wait_recv()

        for parameter in range(9):
            rows = slice(parameter * 8, (parameter + 1) * 8)
            tile, lane = (4, 0) if parameter == 8 else (parameter % 4, parameter // 4 * 64)
            lanes_ref[rows, other * 64 : (other + 1) * 64] = flip_got[other, tile, :, lane : lane + 64]
            tile, lane = (5, 0) if parameter == 8 else (4, 64 + parameter * 8)
            lanes_ref[rows, 512 + other * 8 : 520 + other * 8] = flip_got[other, tile, :, lane : lane + 8]
    lower_ref[...] = lanes_ref[...]


    @pl.when(pt != row)
    def _():
        last_row.wait_send()

    def drain_blocks(other, _):
        for kind in range(2):

            @pl.when(other != pt)
            def _(kind=kind):
                to_middle(kind, other, pt).wait_send()

            @pl.when(other != (row if kind == 0 else mirror))
            def _(kind=kind):
                to_end(kind, other, row).wait_send()

        return 0

    lax.fori_loop(0, 8, drain_blocks, 0)


def order(upper_in, lower_in, upper_ref, lower_ref, perm_ref):
    source = lax.broadcasted_iota(jnp.int32, (WIDTH, WIDTH), 1)
    goal = lax.broadcasted_iota(jnp.int32, (WIDTH, WIDTH), 0)
    perm_ref[...] = jnp.where((source & 63) * 9 + (source >> 6) == goal, 1.0, 0.0).astype(BF16)

    def write_rows(target_ref, value):
        for parameter in range(9):
            for camera in range(8):
                goal_row, source_row = camera * 9 + parameter, parameter * 8 + camera
                target_ref[goal_row : goal_row + 1, :] = value[source_row : source_row + 1]

    write_rows(upper_ref, permute_columns(upper_in[...], perm_ref))
    write_rows(lower_ref, permute_columns(lower_in[...], perm_ref))


def body(jac_cam, jac_pt, obs_cam, point_covisible_tile):
    def rows_of(array):
        observed, _, width, held = array.shape
        array = array.transpose(0, 2, 1, 3).reshape(observed * width, 2, held // LANES, LANES)
        return array.transpose(0, 2, 1, 3).reshape(observed * width * 2 * held // LANES, LANES)

    vmem = pl.BlockSpec(memory_space=pltpu.VMEM)
    upper, lower = pl.pallas_call(
        kernel,
        out_shape=[jax.ShapeDtypeStruct((72, WIDTH), F32)] * 2,
        in_specs=[pl.BlockSpec(memory_space=pl.ANY)] * 4,
        out_specs=[vmem] * 2,
        scratch_shapes=[
            pltpu.VMEM((2304, LANES), F32),
            pltpu.VMEM((768, LANES), F32),
            pltpu.VMEM((8, 2048), jnp.int32),
            pltpu.VMEM((16, LANES), jnp.int32),
            pltpu.VMEM((400, 2048), BF16),
            pltpu.VMEM((768, LANES), F32),
            pltpu.VMEM((512, LANES), BF16),
            pltpu.VMEM((16, LANES), F32),
            pltpu.VMEM((256, 2048), BF16),
            pltpu.VMEM((TILES, FEATURES, LANES), F32),
            pltpu.VMEM((TILES, FEATURES, LANES), F32),
            pltpu.VMEM((18, FEATURES, LANES), F32),
            pltpu.VMEM((WIDTH, 3 * LANES * GROUP), BF16),
            pltpu.VMEM((WIDTH, 3 * LANES * GROUP), BF16),
            pltpu.VMEM((8, 72, WIDTH), F32),
            pltpu.VMEM((4, 72, WIDTH), F32),
            pltpu.VMEM((3, 72, WIDTH), F32),
            pltpu.VMEM((72, WIDTH), F32),
            pltpu.VMEM((LANES, 384), F32),
            pltpu.VMEM((8, 8, WIDTH), F32),
            pltpu.VMEM((9, 8, WIDTH), F32),
            pltpu.VMEM((8, 6, 8, LANES), F32),
            pltpu.VMEM((8, 6, 8, LANES), F32),
            pltpu.VMEM((8, 6, 8, LANES), F32),
            pltpu.VMEM((72, WIDTH), F32),
            pltpu.SemaphoreType.DMA((4,)),
            pltpu.SemaphoreType.DMA((TILES,)),
            pltpu.SemaphoreType.DMA((TILES,)),
            pltpu.SemaphoreType.DMA((18,)),
            pltpu.SemaphoreType.DMA((18,)),
            pltpu.SemaphoreType.DMA((2, 4, CHUNKS)),
            pltpu.SemaphoreType.DMA((2, 4, CHUNKS)),
            pltpu.SemaphoreType.DMA((2, 8)),
            pltpu.SemaphoreType.DMA((2, 8)),
            pltpu.SemaphoreType.DMA((2, 8)),
            pltpu.SemaphoreType.DMA((2, 8)),
            pltpu.SemaphoreType.DMA((2,)),
        ],
        compiler_params=pltpu.CompilerParams(
            collective_id=0, has_side_effects=True, vmem_limit_bytes=64 * 2**20 - 2**19
        ),
    )(rows_of(jac_cam), rows_of(jac_pt), obs_cam, point_covisible_tile.reshape(16, LANES))
    upper, lower = pl.pallas_call(
        order,
        out_shape=[jax.ShapeDtypeStruct((72, WIDTH), F32)] * 2,
        in_specs=[vmem] * 2,
        out_specs=[vmem] * 2,
        scratch_shapes=[pltpu.VMEM((WIDTH, WIDTH), BF16)],
        compiler_params=pltpu.CompilerParams(vmem_limit_bytes=64 * 2**20 - 2**19),
    )(upper, lower)
    return (upper[None], lower[None])


def solution(mesh):
    in_specs = (
        P(None, None, None, ("pt", "row", "col")),
        P(None, None, None, ("pt", "row", "col")),
        P(None, ("pt", "row", "col")),
        P(("pt", "row", "col"), None),
    )
    out_specs = (P(("row", "col"), "pt", None), P(("row", "col"), "pt", None))
    return jax.shard_map(body, mesh=mesh, in_specs=in_specs, out_specs=out_specs, check_vma=False)
```
